768 devices in a mesh: lat: 128 (over x, z_hi, y, core), section: 6 (over z_lo).
Axes of the slice: x: 4, y: 8, z: 12 (z_hi: 2, z_lo: 6; z = z_hi * 6 + z_lo), core: 2. Of those that a mesh axis runs over, the one named last changes fastest.
Arguments:
- trajectory: bfloat16 [6, 2, 1024, 8, 768], P('section', None, 'lat'), may hold values from -8 to 8
- observed: bfloat16 [6, 2, 1024, 8, 768], P('section', None, 'lat'), may hold values from -6 to 6
- obs_mask: int32 [6, 1024, 8], P('section', 'lat'), may hold values 0 or 1
- shift_rows: int32 [6], P('section'), may hold values from 0 to 7
- final_adjoint: float32 [2, 1024, 8, 768], P(None, 'lat'), may hold values from -6 to 6
- w_query: bfloat16 [6, 768, 384], P('section'), may hold values from -0.21875 to 0.21875
- w_key: bfloat16 [6, 768, 384], P('section'), may hold values from -0.21875 to 0.21875
- w_value: bfloat16 [6, 768, 384], P('section'), may hold values from -0.21875 to 0.21875
- w_out: bfloat16 [6, 384, 768], P('section'), may hold values from -0.3125 to 0.3125
Outputs:
- adjoint_field: float32 [6, 2, 1024, 8, 768], P('section', None, 'lat')
The draws below stay inside these ranges and needn't reach their ends.
All inputs are finite; a program needn't handle non-finite values. No bound on the sum of `obs_mask` on one device may be relied on, other than what follows from the above.
Results may differ from the reference program's by a relative error of at most 0.015.
Values may be sent and summed in bfloat16 or wider, within the bound.
No kernel may reach another device: no remote copies, remote signals or barrier semaphores. Data moves between devices by JAX's collectives and lax.ppermute only.
A program may use at most 64 MiB of HBM per device.

```python
import jax
import jax.numpy as jnp
from jax import lax

D = 768
HEADS = 12
HD = 32
WIN = 8
LON = 8
MEMBERS = 2
STEPS = 6
NLAT = 1024


def draw_trajectory(key, part):
    key = jax.random.fold_in(key, 7)
    full_shape = (STEPS, MEMBERS, NLAT, LON, D)
    values = jax.random.truncated_normal(key, -4.0, 4.0, full_shape, jnp.float32)
    return values.astype(jnp.bfloat16)


def touch_ends(result, stream_key, smallest, largest):
    spot = [jax.random.randint(jax.random.fold_in(stream_key, axis), (), 0, length) for axis, length in enumerate(result.shape)]
    widest = result.shape.index(max(result.shape))
    beside = spot[:widest] + [(spot[widest] + 1) % result.shape[widest]] + spot[widest + 1:]
    return result.at[tuple(spot)].set(smallest).at[tuple(beside)].set(largest)


def block_levels(key, dims, pieces, least, largest):
    def one(dim, shards_of):
        heights = jax.random.uniform(jax.random.fold_in(jax.random.fold_in(key, 6), dim), (shards_of,), jnp.float32, least / len(pieces), largest / len(pieces))
        return jnp.repeat(jnp.exp(heights), dims[dim] // shards_of).reshape((-1,) + (1,) * (len(dims) - dim - 1))

    level = one(*pieces[0])
    for cut in pieces[1:]:
        level = level * one(*cut)
    return level


def centred(own_key, extent, scale, most, pieces=(), kind=jnp.bfloat16):
    result = jax.random.normal(own_key, extent, jnp.float32) * scale
    if len(pieces) > 0:
        result = block_levels(own_key, extent, pieces, -0.22, 0.18) * result
    return jnp.clip(result, min=-most, max=most).astype(kind)


def setup_inputs(seed: int = 0) -> dict:
    seeds = jax.random.split(jax.random.key(seed), 10)
    trajectory = draw_trajectory(jax.random.fold_in(seeds[9], 71), 0)
    observed = centred(seeds[1], (STEPS, MEMBERS, NLAT, LON, D), 1.0, 6.0, ((0, 6), (2, 128)))
    obs_mask = touch_ends((jax.random.randint(seeds[2], (STEPS, NLAT, LON), 0, 2) < 1).astype(jnp.int32), jax.random.fold_in(seeds[2], 1), 0, 1)
    shift_rows = touch_ends(jax.random.randint(seeds[3], (STEPS,), 0, WIN), jax.random.fold_in(seeds[3], 1), 0, WIN - 1).astype(jnp.int32)
    final_adjoint = centred(seeds[4], (MEMBERS, NLAT, LON, D), 1.0, 6.0, ((1, 128),), jnp.float32)
    w_query = centred(seeds[5], (STEPS, D, HEADS * HD), D ** -0.5, 0.21875, ((0, 6),))
    w_key = centred(seeds[6], (STEPS, D, HEADS * HD), D ** -0.5, 0.21875, ((0, 6),))
    w_value = centred(seeds[7], (STEPS, D, HEADS * HD), D ** -0.5, 0.21875, ((0, 6),))
    w_out = centred(seeds[8], (STEPS, HEADS * HD, D), (HEADS * HD) ** -0.5, 0.3125, ((0, 6),))
    return {"trajectory": trajectory, "observed": observed, "obs_mask": obs_mask, "shift_rows": shift_rows, "final_adjoint": final_adjoint, "w_query": w_query, "w_key": w_key, "w_value": w_value, "w_out": w_out}


def to_windows(field):
    count, across, width = field.shape
    split = field.reshape(count // WIN, WIN, across // WIN, WIN, width)
    return split.transpose(0, 2, 1, 3, 4).reshape(-1, WIN * WIN, width)


def from_windows(tiles, count, across):
    width = tiles.shape[-1]
    split = tiles.reshape(count // WIN, across // WIN, WIN, WIN, width)
    return split.transpose(0, 2, 1, 3, 4).reshape(count, across, width)


def window_adjoint(tiles, grad_tiles, key_valid, w_query, w_key, w_value, w_out):
    high = lax.Precision.HIGHEST
    flt = jnp.float32
    count, tokens, width = tiles.shape
    hidden = w_query.shape[1]
    head_dim = hidden // HEADS
    scale = head_dim ** -0.5
    tiles_f = tiles.astype(flt)
    queries = (jnp.einsum('wtd,de->wte', tiles_f, w_query.astype(flt), precision=high) * scale).astype(jnp.bfloat16)
    key_rows = jnp.einsum('wtd,de->wte', tiles_f, w_key.astype(flt), precision=high).astype(jnp.bfloat16)
    value_rows = jnp.einsum('wtd,de->wte', tiles_f, w_value.astype(flt), precision=high).astype(jnp.bfloat16)
    heads_q = queries.reshape(count, tokens, HEADS, head_dim).astype(flt)
    heads_k = key_rows.reshape(count, tokens, HEADS, head_dim).astype(flt)
    heads_v = value_rows.reshape(count, tokens, HEADS, head_dim).astype(flt)
    scores = jnp.einsum('wihe,wjhe->whij', heads_q, heads_k, precision=high)
    scores = jnp.where(key_valid[:, None, None, :], scores, -1e9)
    scores = scores - jnp.max(scores, axis=-1, keepdims=True)
    expon = jnp.exp(scores)
    attend = expon / jnp.sum(expon, axis=-1, keepdims=True)
    attend_b = attend.astype(jnp.bfloat16).astype(flt)
    grad_out = jnp.einsum('wid,ed->wie', grad_tiles.astype(flt), w_out.astype(flt), precision=high).astype(jnp.bfloat16)
    heads_g = grad_out.reshape(count, tokens, HEADS, head_dim).astype(flt)
    grad_probs = jnp.einsum('wihe,wjhe->whij', heads_g, heads_v, precision=high)
    grad_scores = attend * (grad_probs - jnp.sum(attend * grad_probs, axis=-1, keepdims=True))
    grad_scores = grad_scores.astype(jnp.bfloat16).astype(flt)
    grad_query = (jnp.einsum('whij,wjhe->wihe', grad_scores, heads_k, precision=high) * scale).astype(jnp.bfloat16)
    grad_key = jnp.einsum('whij,wihe->wjhe', grad_scores, heads_q, precision=high)
    grad_value = jnp.einsum('whij,wihe->wjhe', attend_b, heads_g, precision=high)
    change_q = jnp.einsum('wie,de->wid', grad_query.reshape(count, tokens, hidden).astype(flt), w_query.astype(flt), precision=high)
    grad_both = jnp.concatenate([grad_key.reshape(count, tokens, hidden), grad_value.reshape(count, tokens, hidden)], axis=-1)
    w_both = jnp.concatenate([w_key, w_value], axis=1).astype(flt)
    change_kv = jnp.einsum('wje,de->wjd', grad_both, w_both, precision=high)
    return change_q + change_kv


def reference(trajectory, observed, obs_mask, shift_rows, final_adjoint, w_query, w_key, w_value, w_out):
    steps, members, nlat, across, width = trajectory.shape
    span = nlat + WIN
    row_ids = jnp.arange(nlat + 2 * WIN, dtype=jnp.int32) - WIN
    inside = (row_ids >= 0) & (row_ids < nlat)
    pad_rows = ((WIN, WIN), (0, 0), (0, 0))
    results = []
    for member in range(members):
        adjoint = final_adjoint[member].astype(jnp.float32)
        per_step = [None] * steps
        for section in reversed(range(steps)):
            state = trajectory[section, member]
            offset = shift_rows[section].astype(jnp.int32)
            padded = jnp.pad(state, pad_rows)
            grad_pad = jnp.pad(adjoint.astype(jnp.bfloat16), pad_rows)
            x_span = lax.dynamic_slice_in_dim(padded, offset, span, 0)
            g_span = lax.dynamic_slice_in_dim(grad_pad, offset, span, 0)
            v_span = lax.dynamic_slice_in_dim(inside, offset, span, 0)
            valid_grid = jnp.broadcast_to(v_span[:, None, None], (span, across, 1))
            key_valid = to_windows(valid_grid)[:, :, 0]
            tiles = window_adjoint(to_windows(x_span), to_windows(g_span), key_valid, w_query[section], w_key[section], w_value[section], w_out[section])
            change_span = from_windows(tiles, span, across)
            change = lax.dynamic_update_slice_in_dim(jnp.zeros((nlat + 2 * WIN, across, width), jnp.float32), change_span, offset, 0)
            forcing = obs_mask[section][:, :, None].astype(jnp.float32) * (state.astype(jnp.float32) - observed[section, member].astype(jnp.float32))
            adjoint = adjoint + change[WIN:WIN + nlat] + forcing
            per_step[section] = adjoint
        results.append(jnp.stack(per_step))
    return jnp.stack(results, axis=1)
```

```python
import functools

import jax
import jax.numpy as jnp
from jax import lax
from jax.experimental import pallas as pl
from jax.experimental.pallas import tpu as pltpu
from jax.sharding import PartitionSpec as P

HD = 32
WIN = 8
AXES = ("lat", "section")
FLT = jnp.float32
BF = jnp.bfloat16
BAND = 64
SLOT = 128
GROUP = 4


def dot_nn(a, b):
    return lax.dot_general(a, b, (((1,), (0,)), ((), ())), preferred_element_type=FLT)


def dot_nt(a, b):
    return lax.dot_general(a, b, (((1,), (1,)), ((), ())), preferred_element_type=FLT)


def gathered(rows, field, core, offset, own, other, near0, near1):
    near = jnp.where(core == 0, near0[field].astype(FLT), near1[field].astype(FLT))
    rows[0:BAND, :] = near
    rows[pl.ds(pl.multiple_of(BAND + BAND * core, BAND), BAND), :] = own[core, field].astype(FLT)
    rows[pl.ds(pl.multiple_of(2 * BAND - BAND * core, BAND), BAND), :] = other[field].astype(FLT)
    return rows[pl.ds(pl.multiple_of(offset * WIN, WIN), SLOT), :]


def prepare_kernel(
    fields,
    scalars,
    own,
    other,
    near0,
    near1,
    w_query,
    w_key,
    w_value,
    attend_ref,
    attend_t_ref,
    value_ref,
    key_ref,
    query_t_ref,
    out_ref,
    forcing_ref,
    *rest,
):
    rows = rest[-1]
    core, slot, offset = scalars[0], scalars[1], scalars[2]
    x = gathered(rows, 0, core, offset, own, other, near0, near1).astype(BF)
    forcing_ref[...] = gathered(rows, 1, core, offset, own, other, near0, near1).astype(BF)
    if fields == 3:
        rest[0][...] = gathered(rows, 2, core, offset, own, other, near0, near1).astype(BF)
    scale = HD ** (-0.5)
    q = (dot_nn(x, w_query[...]) * scale).astype(BF)
    k = dot_nn(x, w_key[...]).astype(BF)
    v = dot_nn(x, w_value[...]).astype(BF)
    token = lax.broadcasted_iota(jnp.int32, (SLOT, SLOT), 0)
    other_token = lax.broadcasted_iota(jnp.int32, (SLOT, SLOT), 1)
    row_head = token // HD
    lane_head = other_token // HD
    edge = jnp.where(slot == 0, BAND - offset * WIN, 0)
    allowed = ((token // BAND) == (other_token // BAND)) & (
        (token < edge) == (other_token < edge)
    )
    for group in range(3):
        lanes = slice(SLOT * group, SLOT * group + SLOT)
        q_g, k_g, v_g = q[:, lanes], k[:, lanes], v[:, lanes]
        q_t = q_g.astype(FLT).T
        k_t = k_g.astype(FLT).T
        v_t = v_g.astype(FLT).T
        mixed = jnp.zeros((SLOT, SLOT), FLT)
        for h in range(GROUP):
            at = slice(SLOT * h, SLOT * h + SLOT)
            wide = slice(SLOT * (GROUP * group + h), SLOT * (GROUP * group + h) + SLOT)
            in_rows = row_head == h
            in_lanes = lane_head == h
            scores = dot_nn(q_g, jnp.where(in_rows, k_t, 0.0).astype(BF))
            scores = jnp.where(allowed, scores, -1000000000.0)
            scores = scores - jnp.max(scores, axis=-1, keepdims=True)
            expon = jnp.exp(scores)
            attend = expon / jnp.sum(expon, axis=-1, keepdims=True)
            attend_b = attend.astype(BF)
            attend_ref[:, wide] = attend_b
            attend_t_ref[:, wide] = attend.T.astype(BF)
            mixed += dot_nn(attend_b, jnp.where(in_lanes, v_g, jnp.zeros_like(v_g)))
            value_ref[group, 0:SLOT, at] = jnp.where(in_rows, v_t, 0.0).astype(BF)
            value_ref[group, SLOT : 2 * SLOT, at] = jnp.where(in_rows, -1.0, 0.0).astype(BF)
            key_ref[group, at, :] = jnp.where(in_lanes, k_g, jnp.zeros_like(k_g))
            query_t_ref[group, :, at] = jnp.where(in_rows, q_t, 0.0).astype(BF)
        out_ref[:, lanes] = mixed


def step_kernel(
    first,
    scalars,
    *refs,
):
    if first:
        incoming = refs[:1]
        refs = refs[1:]
    else:
        incoming = refs[:3]
        refs = refs[3:]
    (
        forcing_ref,
        attend_ref,
        attend_t_ref,
        value_ref,
        key_ref,
        query_t_ref,
        out_ref,
        w_query,
        w_key,
        w_value,
        w_out,
        all_ref,
        low_ref,
        high_ref,
        rows,
    ) = refs
    scale = HD ** (-0.5)
    if first:
        adjoint = incoming[0][...].astype(FLT)
    else:
        rows[0:BAND, :] = incoming[0][...].astype(FLT)
        rows[BAND : BAND + SLOT, :] = incoming[1][...].astype(FLT)
        rows[BAND + SLOT :, :] = incoming[2][...].astype(FLT)
        shift = scalars[3]
        adjoint = rows[pl.ds(pl.multiple_of(BAND + shift * WIN, WIN), SLOT), :]
    g = dot_nt(adjoint.astype(BF), w_out[...]).astype(BF)
    lane_head = lax.broadcasted_iota(jnp.int32, (SLOT, SLOT), 1) // HD
    g_query, g_key, g_value = [], [], []
    for group in range(3):
        lanes = slice(SLOT * group, SLOT * group + SLOT)
        wide = slice(GROUP * SLOT * group, GROUP * SLOT * (group + 1))
        g_g = g[:, lanes]
        g_o = (g_g.astype(FLT) * out_ref[:, lanes]).astype(BF)
        centred = dot_nn(jnp.concatenate([g_g, g_o], axis=1), value_ref[group])
        g_s = (attend_ref[:, wide].astype(FLT) * centred).astype(BF)
        g_query.append((dot_nn(g_s, key_ref[group]) * scale).astype(BF))
        stacked = jnp.concatenate(
            [g_s[:, SLOT * h : SLOT * h + SLOT] for h in range(GROUP)], axis=0
        )
        g_key.append(dot_nn(query_t_ref[group], stacked).T.astype(BF))
        spread = jnp.concatenate(
            [jnp.where(lane_head == h, g_g, jnp.zeros_like(g_g)) for h in range(GROUP)], axis=0
        )
        g_value.append(dot_nn(attend_t_ref[:, wide], spread).astype(BF))
    change = dot_nt(jnp.concatenate(g_query, axis=1), w_query[...])
    change += dot_nt(jnp.concatenate(g_key, axis=1), w_key[...])
    change += dot_nt(jnp.concatenate(g_value, axis=1), w_value[...])
    updated = (adjoint + change + forcing_ref[...].astype(FLT)).astype(BF)
    all_ref[...] = updated
    low_ref[...] = updated[:BAND]
    high_ref[...] = updated[BAND:]


def split_kernel(ticks, scalars, *refs):
    results = refs[:ticks]
    own_ref, swap_ref, lower_ref, held, rows, sem = refs[ticks:]
    core, offset, section = scalars[0], scalars[2], scalars[4]
    for tick in range(ticks):

        @pl.when(section == ticks - 1 - tick)
        def _():
            copy = pltpu.make_async_copy(results[tick], held, sem)
            copy.start()
            copy.wait()

    lower_ref[...] = held[0:BAND]
    rows[...] = held[...].astype(FLT)
    even = rows[pl.ds(pl.multiple_of(BAND - offset * WIN, WIN), BAND), :].astype(BF)
    odd = held[BAND:SLOT]
    own_ref[...] = jnp.where(core == 0, even, odd)
    swap_ref[...] = jnp.where(core == 0, odd, even)


def final_kernel(scalars, own, other, near0, near1, result, rows):
    core, offset = scalars[0], scalars[2]
    for member, near in ((0, near0), (1, near1)):
        rows[0:BAND, :] = jnp.where(core == member, own[...].astype(FLT), other[...].astype(FLT))
        rows[BAND:SLOT, :] = near[...].astype(FLT)
        start = jnp.where(core == 1, BAND - offset * WIN, 0)
        result[member] = rows[pl.ds(pl.multiple_of(start, WIN), BAND), :]


def vmem(count):
    return [pl.BlockSpec(memory_space=pltpu.VMEM)] * count


SMEM = pl.BlockSpec(memory_space=pltpu.SMEM)
PARAMS = pltpu.CompilerParams(vmem_limit_bytes=40 * 1024 * 1024)


def struct(shape, kind=BF):
    return jax.ShapeDtypeStruct(shape, kind)


def prepare(scalars, own, other, near0, near1, w_query, w_key, w_value):
    fields, _, width = other.shape
    hidden = w_query.shape[1]
    keys = hidden // HD * SLOT
    shapes = [
        struct((SLOT, keys)),
        struct((SLOT, keys)),
        struct((3, 2 * SLOT, GROUP * SLOT)),
        struct((3, GROUP * SLOT, SLOT)),
        struct((3, SLOT, GROUP * SLOT)),
        struct((SLOT, hidden), FLT),
        struct((SLOT, width)),
    ]
    if fields == 3:
        shapes.append(struct((SLOT, width)))
    return pl.pallas_call(
        functools.partial(prepare_kernel, fields),
        out_shape=shapes,
        in_specs=[SMEM] + vmem(7),
        out_specs=vmem(len(shapes)),
        scratch_shapes=[pltpu.VMEM((3 * BAND, width), FLT)],
        compiler_params=PARAMS,
        name="prepare",
    )(scalars, own, other, near0, near1, w_query, w_key, w_value)


def step(first, scalars, incoming, prepared, weights):
    width = incoming[0].shape[-1]
    attend, attend_t, values, keys, queries_t, out, forcing = prepared
    operands = (*incoming, forcing, attend, attend_t, values, keys, queries_t, out, *weights)
    return pl.pallas_call(
        functools.partial(step_kernel, first),
        out_shape=[struct((SLOT, width)), struct((BAND, width)), struct((BAND, width))],
        in_specs=[SMEM] + vmem(len(operands)),
        out_specs=vmem(3),
        scratch_shapes=[pltpu.VMEM((4 * BAND, width), FLT)],
        compiler_params=PARAMS,
        name="step",
    )(scalars, *operands)


def on_device(
    trajectory, observed, obs_mask, shift_rows, final_adjoint, w_query, w_key, w_value, w_out
):
    sections = lax.axis_size("section")
    bands = lax.axis_size("lat")
    chips = bands // 2
    section_at = lax.axis_index("section")
    band_at = lax.axis_index("lat")
    members, rows_here, across, width = trajectory.shape[1:]
    offset = shift_rows[0].astype(jnp.int32)
    core, chip = band_at % 2, band_at // 2
    weights = (w_query[0], w_key[0], w_value[0], w_out[0])

    def at(band, section):
        return (band % bands) * sections + section

    def sent(value, hops):
        return lax.ppermute(value, AXES, hops)

    def exchange(fields, among):
        both = [(at(b, s), at(b ^ 1, s)) for b in range(bands) for s in among]
        up0 = [(at(2 * j + 1, s), at(2 * j + 2, s)) for j in range(chips) for s in among]
        up1 = [(at(2 * j + 1, s), at(2 * j + 3, s)) for j in range(chips) for s in among]
        near0 = sent(fields[0], up0)
        near1 = sent(fields[1], up1)
        other = sent(lax.dynamic_index_in_dim(fields, 1 - core, 0, keepdims=False), both)
        return other, near0, near1

    x = trajectory[0].reshape(members, BAND, width)
    seen = observed[0].reshape(members, BAND, width)
    weight = obs_mask[0].reshape(1, BAND, 1).astype(FLT)
    forcing = (weight * (x.astype(FLT) - seen.astype(FLT))).astype(BF)
    final = final_adjoint.reshape(members, BAND, width).astype(BF)
    with jax.named_scope("first_exchange"):
        last = jnp.stack([x, forcing, final], axis=1)
        got = exchange(last, [sections - 1])
        above = lax.ppermute(
            shift_rows, "section", [(s, s - 1) for s in range(1, sections)]
        )[0].astype(jnp.int32)
    shift = jnp.where(section_at == sections - 1, 0, offset - above)
    scalars = jnp.stack([core, chip, offset, shift, section_at]).astype(jnp.int32)
    *prepared, start = prepare(scalars, last, *got, *weights[:3])

    result = step(True, scalars, (start,), prepared, weights)
    results = [result[0]]
    with jax.named_scope("later_exchange"):
        pair = jnp.stack([x, forcing], axis=1)
        pair, _ = lax.optimization_barrier((pair, prepared[0]))
        got = exchange(pair, list(range(sections - 1)))
    prepared = prepare(scalars, pair, *got, *weights[:3])
    for tick in range(1, sections):
        source = sections - tick
        with jax.named_scope("pass_on"):
            hops = [
                [(at(b + 2 * way, source), at(b, source - 1)) for b in range(bands)]
                for way in (-1, 1, 0)
            ]
            from_low = sent(result[2], hops[0])
            from_high = sent(result[1], hops[1])
            middle = sent(result[0], hops[2])
        result = step(False, scalars, (from_low, middle, from_high), prepared, weights)
        results.append(result[0])

    own, swap, lower = pl.pallas_call(
        functools.partial(split_kernel, sections),
        out_shape=[struct((BAND, width))] * 3,
        in_specs=[SMEM] + [pl.BlockSpec(memory_space=pl.ANY)] * sections,
        out_specs=vmem(3),
        scratch_shapes=[
            pltpu.VMEM((SLOT, width), BF),
            pltpu.VMEM((SLOT, width), FLT),
            pltpu.SemaphoreType.DMA,
        ],
        compiler_params=PARAMS,
        name="split",
    )(scalars, *results)
    with jax.named_scope("last_exchange"):
        every = range(sections)
        near0 = sent(lower, [(at(2 * j + 2, s), at(2 * j + 1, s)) for j in range(chips) for s in every])
        near1 = sent(lower, [(at(2 * j + 3, s), at(2 * j + 1, s)) for j in range(chips) for s in every])
        other = sent(swap, [(at(b, s), at(b ^ 1, s)) for b in range(bands) for s in every])
    field = pl.pallas_call(
        final_kernel,
        out_shape=struct((members, BAND, width), FLT),
        in_specs=[SMEM] + vmem(4),
        out_specs=vmem(1)[0],
        scratch_shapes=[pltpu.VMEM((SLOT, width), FLT)],
        compiler_params=PARAMS,
        name="merge",
    )(scalars, own, other, near0, near1)
    return field.reshape(1, members, rows_here, across, width)


def solution(mesh):
    placed = (
        P("section", None, "lat", None, None),
        P("section", None, "lat", None, None),
        P("section", "lat", None),
        P("section"),
        P(None, "lat", None, None),
        P("section", None, None),
        P("section", None, None),
        P("section", None, None),
        P("section", None, None),
    )
    return jax.shard_map(
        on_device,
        mesh=mesh,
        in_specs=placed,
        out_specs=P("section", None, "lat", None, None),
        check_vma=False,
    )
```

```python
import functools

import jax
import jax.numpy as jnp
from jax import lax
from jax.experimental import pallas as pl
from jax.experimental.pallas import tpu as pltpu
from jax.sharding import PartitionSpec as P

HD = 32
WIN = 8
AXES = ("lat", "section")
FLT = jnp.float32
BF = jnp.bfloat16
BAND = 64
SLOT = 128
GROUP = 4


def dot_nn(a, b):
    return lax.dot_general(a, b, (((1,), (0,)), ((), ())), preferred_element_type=FLT)


def dot_nt(a, b):
    return lax.dot_general(a, b, (((1,), (1,)), ((), ())), preferred_element_type=FLT)


def near_of(core, near0, near1, field):
    return jnp.where(core == 0, near0[field].astype(FLT), near1[field].astype(FLT))


def gathered(rows, field, core, offset, own, other, near0, near1):
    rows[0:BAND, :] = near_of(core, near0, near1, field)
    rows[pl.ds(pl.multiple_of(BAND + BAND * core, BAND), BAND), :] = own[core, field].astype(FLT)
    rows[pl.ds(pl.multiple_of(2 * BAND - BAND * core, BAND), BAND), :] = other[field].astype(FLT)
    return rows[pl.ds(pl.multiple_of(offset * WIN, WIN), SLOT), :]


def gathered_above(rows, core, offset, own, other, next0, next1):
    rows[0:BAND, :] = jnp.where(core == 1, own[core, 0].astype(FLT), other[0].astype(FLT))
    rows[BAND : 2 * BAND, :] = near_of(core, next0, next1, 0)
    rows[2 * BAND :, :] = jnp.zeros_like(rows[2 * BAND :, :])
    return rows[pl.ds(pl.multiple_of(offset * WIN, WIN), SLOT), :]


def prepare_kernel(
    above,
    with_forcing,
    edge_slot,
    scalars,
    own,
    other,
    near0,
    near1,
    w_query,
    w_key,
    w_value,
    attend_ref,
    attend_t_ref,
    value_ref,
    key_ref,
    query_t_ref,
    out_ref,
    *rest,
):
    rows = rest[-1]
    core, slot, offset = scalars[0], scalars[1], scalars[2]
    if above:
        x = gathered_above(rows, core, offset, own, other, near0, near1).astype(BF)
    else:
        x = gathered(rows, 0, core, offset, own, other, near0, near1).astype(BF)
    if with_forcing:
        rest[0][...] = gathered(rows, 1, core, offset, own, other, near0, near1).astype(BF)
    scale = HD ** (-0.5)
    q = (dot_nn(x, w_query[...]) * scale).astype(BF)
    k = dot_nn(x, w_key[...]).astype(BF)
    v = dot_nn(x, w_value[...]).astype(BF)
    token = lax.broadcasted_iota(jnp.int32, (SLOT, SLOT), 0)
    other_token = lax.broadcasted_iota(jnp.int32, (SLOT, SLOT), 1)
    row_head = token // HD
    lane_head = other_token // HD
    edge = jnp.where(slot == edge_slot, BAND - offset * WIN, 0)
    allowed = ((token // BAND) == (other_token // BAND)) & (
        (token < edge) == (other_token < edge)
    )
    for group in range(3):
        lanes = slice(SLOT * group, SLOT * group + SLOT)
        q_g, k_g, v_g = q[:, lanes], k[:, lanes], v[:, lanes]
        q_t = q_g.astype(FLT).T
        k_t = k_g.astype(FLT).T
        v_t = v_g.astype(FLT).T
        mixed = jnp.zeros((SLOT, SLOT), FLT)
        for h in range(GROUP):
            at = slice(SLOT * h, SLOT * h + SLOT)
            wide = slice(SLOT * (GROUP * group + h), SLOT * (GROUP * group + h) + SLOT)
            in_rows = row_head == h
            in_lanes = lane_head == h
            scores = dot_nn(q_g, jnp.where(in_rows, k_t, 0.0).astype(BF))
            scores = jnp.where(allowed, scores, -1000000000.0)
            scores = scores - jnp.max(scores, axis=-1, keepdims=True)
            expon = jnp.exp(scores)
            attend = expon / jnp.sum(expon, axis=-1, keepdims=True)
            attend_b = attend.astype(BF)
            attend_ref[:, wide] = attend_b
            attend_t_ref[:, wide] = attend.T.astype(BF)
            mixed += dot_nn(attend_b, jnp.where(in_lanes, v_g, jnp.zeros_like(v_g)))
            value_ref[group, 0:SLOT, at] = jnp.where(in_rows, v_t, 0.0).astype(BF)
            value_ref[group, SLOT : 2 * SLOT, at] = jnp.where(in_rows, -1.0, 0.0).astype(BF)
            key_ref[group, at, :] = jnp.where(in_lanes, k_g, jnp.zeros_like(k_g))
            query_t_ref[group, :, at] = jnp.where(in_rows, q_t, 0.0).astype(BF)
        out_ref[:, lanes] = mixed


def changed(adjoint, units, w_query, w_key, w_value, w_out):
    scale = HD ** (-0.5)
    g = dot_nt(adjoint.astype(BF), w_out[...]).astype(BF)
    lane_head = lax.broadcasted_iota(jnp.int32, (SLOT, SLOT), 1) // HD
    g_query, g_key, g_value = [], [], []
    for unit, (attend, attend_t, values, keys, queries_t, out) in enumerate(units):
        tokens = slice(SLOT * unit, SLOT * unit + SLOT)
        for group in range(3):
            lanes = slice(SLOT * group, SLOT * group + SLOT)
            wide = slice(GROUP * SLOT * group, GROUP * SLOT * (group + 1))
            g_g = g[tokens, lanes]
            g_o = (g_g.astype(FLT) * out[:, lanes]).astype(BF)
            centred = dot_nn(jnp.concatenate([g_g, g_o], axis=1), values[group])
            g_s = (attend[:, wide].astype(FLT) * centred).astype(BF)
            g_query.append((dot_nn(g_s, keys[group]) * scale).astype(BF))
            stacked = jnp.concatenate(
                [g_s[:, SLOT * h : SLOT * h + SLOT] for h in range(GROUP)], axis=0
            )
            g_key.append(dot_nn(queries_t[group], stacked).T.astype(BF))
            spread = jnp.concatenate(
                [jnp.where(lane_head == h, g_g, jnp.zeros_like(g_g)) for h in range(GROUP)],
                axis=0,
            )
            g_value.append(dot_nn(attend_t[:, wide], spread).astype(BF))

    def whole(parts):
        slots = [jnp.concatenate(parts[3 * u : 3 * u + 3], axis=1) for u in range(len(units))]
        return jnp.concatenate(slots, axis=0)

    change = dot_nt(whole(g_query), w_query[...])
    change += dot_nt(whole(g_key), w_key[...])
    change += dot_nt(whole(g_value), w_value[...])
    return change


def first_kernel(scalars, own, other, near0, near1, *refs):
    prepared, weights = refs[:6], refs[6:10]
    all_ref, low_ref, high_ref, rows = refs[10:]
    core, offset = scalars[0], scalars[2]
    adjoint = gathered(rows, 0, core, offset, own, other, near0, near1)
    forcing = gathered(rows, 1, core, offset, own, other, near0, near1)
    updated = (adjoint + changed(adjoint, [prepared], *weights) + forcing).astype(BF)
    all_ref[...] = updated
    low_ref[...] = updated[:BAND]
    high_ref[...] = updated[BAND:]


def step_kernel(scalars, low, middle, high, *refs):
    prepared, forcing, weights = refs[:6], refs[6], refs[7:11]
    all_ref, low_ref, high_ref, rows = refs[11:]
    rows[0:BAND, :] = low[...].astype(FLT)
    rows[BAND : BAND + SLOT, :] = middle[...].astype(FLT)
    rows[BAND + SLOT :, :] = high[...].astype(FLT)
    shift = scalars[4]
    adjoint = rows[pl.ds(pl.multiple_of(BAND + shift * WIN, WIN), SLOT), :]
    change = changed(adjoint, [prepared], *weights)
    updated = (adjoint + change + forcing[...].astype(FLT)).astype(BF)
    all_ref[...] = updated
    low_ref[...] = updated[:BAND]
    high_ref[...] = updated[BAND:]


def last_kernel(scalars, low, middle, high, *refs):
    units, weights = [refs[:6], refs[6:12]], refs[12:16]
    own_ref, swap_ref, rows = refs[16:]
    rows[0:BAND, :] = low[...].astype(FLT)
    rows[BAND : BAND + SLOT, :] = middle[...].astype(FLT)
    rows[BAND + SLOT : BAND + 2 * SLOT, :] = high[...].astype(FLT)
    rows[BAND + 2 * SLOT :, :] = jnp.zeros_like(rows[BAND + 2 * SLOT :, :])
    core, offset, shift = scalars[0], scalars[2], scalars[4]
    adjoint = rows[pl.ds(pl.multiple_of(BAND + shift * WIN, WIN), 2 * SLOT), :]
    rows[0 : 2 * SLOT, :] = adjoint + changed(adjoint, units, *weights)
    even = rows[pl.ds(pl.multiple_of(BAND - offset * WIN, WIN), BAND), :].astype(BF)
    odd = rows[pl.ds(pl.multiple_of(2 * BAND - offset * WIN, WIN), BAND), :].astype(BF)
    own_ref[...] = jnp.where(core == 0, even, odd)
    swap_ref[...] = jnp.where(core == 0, odd, even)


def split_kernel(scalars, *refs):
    results = refs[:-6]
    own_ref, swap_ref, lower_ref, held, rows, sem = refs[-6:]
    core, offset, section = scalars[0], scalars[2], scalars[3]
    for tick, result in enumerate(results):

        @pl.when(section == len(results) - tick)
        def _():
            copy = pltpu.make_async_copy(result, held, sem)
            copy.start()
            copy.wait()

    lower_ref[...] = held[0:BAND]
    rows[...] = held[...].astype(FLT)
    even = rows[pl.ds(pl.multiple_of(BAND - offset * WIN, WIN), BAND), :].astype(BF)
    odd = held[BAND:SLOT]
    own_ref[...] = jnp.where(core == 0, even, odd)
    swap_ref[...] = jnp.where(core == 0, odd, even)


def merge_kernel(
    scalars, own, other, near0, near1, own_last, other_last, forcing, result, rows
):
    core, offset, section = scalars[0], scalars[2], scalars[3]

    @pl.when(section == 0)
    def _():
        for member in range(2):
            mine = jnp.where(
                core == member, own_last[...].astype(FLT), other_last[...].astype(FLT)
            )
            result[member] = mine + forcing[member].astype(FLT)

    @pl.when(section != 0)
    def _():
        for member, near in ((0, near0), (1, near1)):
            rows[0:BAND, :] = jnp.where(
                core == member, own[...].astype(FLT), other[...].astype(FLT)
            )
            rows[BAND:SLOT, :] = near[...].astype(FLT)
            start = jnp.where(core == 1, BAND - offset * WIN, 0)
            result[member] = rows[pl.ds(pl.multiple_of(start, WIN), BAND), :]


def struct(shape, kind=BF):
    return jax.ShapeDtypeStruct(shape, kind)


SMEM = pl.BlockSpec(memory_space=pltpu.SMEM)
VMEM = pl.BlockSpec(memory_space=pltpu.VMEM)
ANY = pl.BlockSpec(memory_space=pl.ANY)


def call(name, kernel, scalars, operands, shapes, scratch, place=VMEM):
    return pl.pallas_call(
        kernel,
        out_shape=shapes,
        in_specs=[SMEM] + [place] * len(operands),
        out_specs=[VMEM] * len(shapes),
        scratch_shapes=scratch,
        compiler_params=pltpu.CompilerParams(vmem_limit_bytes=40 * 1024 * 1024),
        name=name,
    )(scalars, *operands)


def prepare(scalars, operands, weights, edge_slot, above=False, with_forcing=False):
    width, hidden = weights[0].shape
    keys = hidden // HD * SLOT
    shapes = [
        struct((SLOT, keys)),
        struct((SLOT, keys)),
        struct((3, 2 * SLOT, GROUP * SLOT)),
        struct((3, GROUP * SLOT, SLOT)),
        struct((3, SLOT, GROUP * SLOT)),
        struct((SLOT, hidden), FLT),
    ]
    if with_forcing:
        shapes.append(struct((SLOT, width)))
    return call(
        "prepare",
        functools.partial(prepare_kernel, above, with_forcing, edge_slot),
        scalars,
        (*operands, *weights[:3]),
        shapes,
        [pltpu.VMEM((3 * BAND, width), FLT)],
    )


def on_device(
    trajectory, observed, obs_mask, shift_rows, final_adjoint, w_query, w_key, w_value, w_out
):
    sections = lax.axis_size("section")
    bands = lax.axis_size("lat")
    chips = bands // 2
    section_at = lax.axis_index("section")
    band_at = lax.axis_index("lat")
    members, rows_here, across, width = trajectory.shape[1:]
    offset = shift_rows[0].astype(jnp.int32)
    core, chip = band_at % 2, band_at // 2
    weights = (w_query[0], w_key[0], w_value[0], w_out[0])

    def at(band, section):
        return (band % bands) * sections + section

    def sent(value, hops):
        return lax.ppermute(value, AXES, hops)

    def moved(ways, among):
        return [(at(a, s), at(b, s)) for a, b in ways for s in among]

    def exchange(fields, among):
        near0 = sent(fields[0], moved([(2 * j + 1, 2 * j + 2) for j in range(chips)], among))
        near1 = sent(fields[1], moved([(2 * j + 1, 2 * j + 3) for j in range(chips)], among))
        other = sent(
            lax.dynamic_index_in_dim(fields, 1 - core, 0, keepdims=False),
            moved([(b, b ^ 1) for b in range(bands)], among),
        )
        return other, near0, near1

    def flat(values):
        return values.reshape(members, 1, BAND, width)

    def ints(*values):
        return jnp.stack(values).astype(jnp.int32)

    final_section = [sections - 1]
    x = flat(trajectory[0])
    with jax.named_scope("first_states"):
        first_x = exchange(x, final_section)
    weight = obs_mask[0].reshape(1, 1, BAND, 1).astype(FLT)
    forcing = (weight * (x.astype(FLT) - flat(observed[0]).astype(FLT))).astype(BF)
    final = flat(final_adjoint).astype(BF)
    with jax.named_scope("first_adjoint"):
        begin = jnp.concatenate([final, forcing], axis=1)
        begin, _ = lax.optimization_barrier((begin, first_x[0]))
        first_begin = exchange(begin, final_section)
    with jax.named_scope("shifts"):
        down = [(s, s - 1) for s in range(1, sections)]
        above = lax.ppermute(shift_rows, "section", down)[0].astype(jnp.int32)
    shift = jnp.where(section_at == sections - 1, 0, offset - above)
    place = ints(core, chip, offset, section_at, shift)

    prepared = prepare(place, (x, *first_x), weights, 0)
    result = call(
        "first_step",
        first_kernel,
        place,
        (begin, *first_begin, *prepared, *weights),
        [struct((SLOT, width)), struct((BAND, width)), struct((BAND, width))],
        [pltpu.VMEM((3 * BAND, width), FLT)],
    )
    results = [result[0]]
    with jax.named_scope("later_states"):
        pair = jnp.concatenate([x, forcing], axis=1)
        pair, _ = lax.optimization_barrier((pair, prepared[0]))
        later = exchange(pair, list(range(sections - 1)))
    *prepared, forcing_here = prepare(place, (pair, *later), weights, 0, with_forcing=True)
    for tick in range(1, sections):
        source = sections - tick
        whole, low, high = result

        def across_from(way):
            return [(at(b + 2 * way, source), at(b, source - 1)) for b in range(bands)]

        with jax.named_scope("pass_on"):
            if tick == sections - 1:
                from_low = sent(high, across_from(-1))
                from_high = sent(whole, across_from(1))
                middle = sent(whole, across_from(0))
            else:
                from_low = sent(high, across_from(-1))
                from_high = sent(low, across_from(1))
                middle = sent(whole, across_from(0))
        if tick == sections - 1:
            break
        result = call(
            "step",
            step_kernel,
            place,
            (from_low, middle, from_high, *prepared, forcing_here, *weights),
            [struct((SLOT, width)), struct((BAND, width)), struct((BAND, width))],
            [pltpu.VMEM((4 * BAND, width), FLT)],
        )
        results.append(result[0])

    with jax.named_scope("window_above"):
        ups = [(2 * j + 2, 2 * j) for j in range(chips)], [(2 * j + 2, 2 * j + 1) for j in range(chips)]
        next0 = sent(x[0], moved(ups[0], [0]))
        next1 = sent(x[1], moved(ups[1], [0]))
        extra = prepare(place, (pair, later[0], next0, next1), weights, chips - 1, above=True)
    own, swap, lower = call(
        "split",
        split_kernel,
        place,
        results,
        [struct((BAND, width))] * 3,
        [
            pltpu.VMEM((SLOT, width), BF),
            pltpu.VMEM((SLOT, width), FLT),
            pltpu.SemaphoreType.DMA,
        ],
        place=ANY,
    )
    with jax.named_scope("earlier_results"):
        every = range(1, sections)
        near0 = sent(lower, moved([(2 * j + 2, 2 * j + 1) for j in range(chips)], every))
        near1 = sent(lower, moved([(2 * j + 3, 2 * j + 1) for j in range(chips)], every))
        other = sent(swap, moved([(b, b ^ 1) for b in range(bands)], every))
    own_last, swap_last = call(
        "last_step",
        last_kernel,
        place,
        (from_low, middle, from_high, *prepared, *extra, *weights),
        [struct((BAND, width))] * 2,
        [pltpu.VMEM((6 * BAND, width), FLT)],
    )
    with jax.named_scope("last_result"):
        other_last = sent(swap_last, moved([(b, b ^ 1) for b in range(bands)], [0]))
    (field,) = call(
        "merge",
        merge_kernel,
        place,
        (own, other, near0, near1, own_last, other_last, forcing.reshape(members, BAND, width)),
        [struct((members, BAND, width), FLT)],
        [pltpu.VMEM((SLOT, width), FLT)],
    )
    return field.reshape(1, members, rows_here, across, width)


def solution(mesh):
    placed = (
        P("section", None, "lat", None, None),
        P("section", None, "lat", None, None),
        P("section", "lat", None),
        P("section"),
        P(None, "lat", None, None),
        P("section", None, None),
        P("section", None, None),
        P("section", None, None),
        P("section", None, None),
    )
    return jax.shard_map(
        on_device,
        mesh=mesh,
        in_specs=placed,
        out_specs=P("section", None, "lat", None, None),
        check_vma=False,
    )
```

```python
import functools

import jax
import jax.numpy as jnp
from jax import lax
from jax.experimental import pallas as pl
from jax.experimental.pallas import tpu as pltpu
from jax.sharding import PartitionSpec as P

HD = 32
WIN = 8
AXES = ("lat", "section")
FLT = jnp.float32
BF = jnp.bfloat16
BAND = 64
SLOT = 128
GROUP = 4
RUN = 8


def dot_nn(a, b):
    return lax.dot_general(a, b, (((1,), (0,)), ((), ())), preferred_element_type=FLT)


def dot_nt(a, b):
    return lax.dot_general(a, b, (((1,), (1,)), ((), ())), preferred_element_type=FLT)


def near_of(core, near0, near1, field):
    return jnp.where(core == 0, near0[field].astype(FLT), near1[field].astype(FLT))


def gathered(rows, scalars, own, other, near0, near1, field):
    core, offset, lift = scalars[0], scalars[2], scalars[4]

    def place(token, value):
        rows[pl.ds(pl.multiple_of(token, BAND), BAND), :] = value.astype(FLT)

    base = BAND * (1 - lift)
    place(2 * BAND * lift, near_of(core, near0, near1, field))
    place(base + BAND * core, own[core, field])
    place(base + BAND * (1 - core), other[field])
    return rows[pl.ds(pl.multiple_of(offset * WIN, WIN), SLOT), :]


def gathered_above(rows, core, offset, own, other, next0, next1):
    rows[0:BAND, :] = jnp.where(core == 1, own[core, 0].astype(FLT), other[0].astype(FLT))
    rows[BAND : 2 * BAND, :] = near_of(core, next0, next1, 0)
    rows[2 * BAND :, :] = jnp.zeros_like(rows[2 * BAND :, :])
    return rows[pl.ds(pl.multiple_of(offset * WIN, WIN), SLOT), :]


def prepare_kernel(
    above,
    with_forcing,
    last_slot,
    scalars,
    own,
    other,
    near0,
    near1,
    w_query,
    w_key,
    w_value,
    attend_ref,
    attend_t_ref,
    value_ref,
    key_ref,
    query_t_ref,
    out_ref,
    *rest,
):
    rows = rest[-1]
    core, slot, offset = scalars[0], scalars[1], scalars[2]
    if above:
        x = gathered_above(rows, core, offset, own, other, near0, near1).astype(BF)
    else:
        x = gathered(rows, scalars, own, other, near0, near1, 0).astype(BF)
    if with_forcing:
        rest[0][...] = gathered(rows, scalars, own, other, near0, near1, 1).astype(BF)
    scale = HD ** (-0.5)
    q = (dot_nn(x, w_query[...]) * scale).astype(BF)
    k = dot_nn(x, w_key[...]).astype(BF)
    v = dot_nn(x, w_value[...]).astype(BF)
    token = lax.broadcasted_iota(jnp.int32, (SLOT, SLOT), 0)
    other_token = lax.broadcasted_iota(jnp.int32, (SLOT, SLOT), 1)
    row_head = token // HD
    lane_head = other_token // HD
    start = BAND - offset * WIN
    if above:
        edge = jnp.where(slot == last_slot, start, 0)
    else:
        lift = scalars[4]
        edge_slot = jnp.where(lift == 0, 0, last_slot)
        edge = jnp.where(slot == edge_slot, start + BAND * lift, 0)
    allowed = ((token // BAND) == (other_token // BAND)) & (
        (token < edge) == (other_token < edge)
    )
    for group in range(3):
        lanes = slice(SLOT * group, SLOT * group + SLOT)
        q_g, k_g, v_g = q[:, lanes], k[:, lanes], v[:, lanes]
        q_t = q_g.astype(FLT).T
        k_t = k_g.astype(FLT).T
        v_t = v_g.astype(FLT).T
        mixed = jnp.zeros((SLOT, SLOT), FLT)
        for h in range(GROUP):
            at = slice(SLOT * h, SLOT * h + SLOT)
            wide = slice(SLOT * (GROUP * group + h), SLOT * (GROUP * group + h) + SLOT)
            in_rows = row_head == h
            in_lanes = lane_head == h
            scores = dot_nn(q_g, jnp.where(in_rows, k_t, 0.0).astype(BF))
            scores = jnp.where(allowed, scores, -1000000000.0)
            scores = scores - jnp.max(scores, axis=-1, keepdims=True)
            expon = jnp.exp(scores)
            attend = expon / jnp.sum(expon, axis=-1, keepdims=True)
            attend_b = attend.astype(BF)
            attend_ref[:, wide] = attend_b
            attend_t_ref[:, wide] = attend.T.astype(BF)
            mixed += dot_nn(attend_b, jnp.where(in_lanes, v_g, jnp.zeros_like(v_g)))
            value_ref[group, 0:SLOT, at] = jnp.where(in_rows, v_t, 0.0).astype(BF)
            value_ref[group, SLOT : 2 * SLOT, at] = jnp.where(in_rows, -1.0, 0.0).astype(BF)
            key_ref[group, at, :] = jnp.where(in_lanes, k_g, jnp.zeros_like(k_g))
            query_t_ref[group, :, at] = jnp.where(in_rows, q_t, 0.0).astype(BF)
        out_ref[:, lanes] = mixed


def changed(adjoint, units, w_query, w_key, w_value, w_out):
    scale = HD ** (-0.5)
    g = dot_nt(adjoint.astype(BF), w_out[...]).astype(BF)
    lane_head = lax.broadcasted_iota(jnp.int32, (SLOT, SLOT), 1) // HD
    g_query, g_key, g_value = [], [], []
    for unit, (attend, attend_t, values, keys, queries_t, out) in enumerate(units):
        tokens = slice(SLOT * unit, SLOT * unit + SLOT)
        for group in range(3):
            lanes = slice(SLOT * group, SLOT * group + SLOT)
            wide = slice(GROUP * SLOT * group, GROUP * SLOT * (group + 1))
            g_g = g[tokens, lanes]
            g_o = (g_g.astype(FLT) * out[:, lanes]).astype(BF)
            centred = dot_nn(jnp.concatenate([g_g, g_o], axis=1), values[group])
            g_s = (attend[:, wide].astype(FLT) * centred).astype(BF)
            g_query.append((dot_nn(g_s, keys[group]) * scale).astype(BF))
            stacked = jnp.concatenate(
                [g_s[:, SLOT * h : SLOT * h + SLOT] for h in range(GROUP)], axis=0
            )
            g_key.append(dot_nn(queries_t[group], stacked).T.astype(BF))
            spread = jnp.concatenate(
                [jnp.where(lane_head == h, g_g, jnp.zeros_like(g_g)) for h in range(GROUP)],
                axis=0,
            )
            g_value.append(dot_nn(attend_t[:, wide], spread).astype(BF))

    def whole(parts):
        slots = [jnp.concatenate(parts[3 * u : 3 * u + 3], axis=1) for u in range(len(units))]
        return jnp.concatenate(slots, axis=0)

    change = dot_nt(whole(g_query), w_query[...])
    change += dot_nt(whole(g_key), w_key[...])
    change += dot_nt(whole(g_value), w_value[...])
    return change


def first_kernel(scalars, own, final, other, final_other, near0, near1, final0, final1, *refs):
    prepared, weights = refs[:6], refs[6:10]
    all_ref, rows = refs[10:]
    forcing = gathered(rows, scalars, own, other, near0, near1, 1)
    adjoint = gathered(rows, scalars, final, final_other, final0, final1, 0)
    all_ref[...] = (adjoint + changed(adjoint, [prepared], *weights) + forcing).astype(BF)


def step_kernel(scalars, above, low, high, *refs):
    prepared, forcing, weights = refs[:6], refs[6], refs[7:11]
    outs, rows = refs[11:-1], refs[-1]
    rows[0:SLOT, :] = low[...].astype(FLT)
    rows[SLOT:, :] = high[...].astype(FLT)
    start = BAND + (scalars[2] - above[0]) * WIN
    adjoint = rows[pl.ds(pl.multiple_of(start, WIN), SLOT), :]
    change = changed(adjoint, [prepared], *weights)
    updated = (adjoint + change + forcing[...].astype(FLT)).astype(BF)
    outs[0][...] = updated
    if len(outs) == 2:
        outs[1][...] = updated[BAND:]


def last_kernel(scalars, above, low, middle, high, *refs):
    units, weights = [refs[:6], refs[6:12]], refs[12:16]
    own_ref, swap_ref, rows = refs[16:]
    rows[0:BAND, :] = low[...].astype(FLT)
    rows[BAND : BAND + SLOT, :] = middle[...].astype(FLT)
    rows[BAND + SLOT : BAND + 2 * SLOT, :] = high[...].astype(FLT)
    rows[BAND + 2 * SLOT :, :] = jnp.zeros_like(rows[BAND + 2 * SLOT :, :])
    core, offset = scalars[0], scalars[2]
    shift = offset - above[0]
    adjoint = rows[pl.ds(pl.multiple_of(BAND + shift * WIN, WIN), 2 * SLOT), :]
    rows[0 : 2 * SLOT, :] = adjoint + changed(adjoint, units, *weights)
    even = rows[pl.ds(pl.multiple_of(BAND - offset * WIN, WIN), BAND), :].astype(BF)
    odd = rows[pl.ds(pl.multiple_of(2 * BAND - offset * WIN, WIN), BAND), :].astype(BF)
    own_ref[...] = jnp.where(core == 0, even, odd)
    swap_ref[...] = jnp.where(core == 0, odd, even)


def split_kernel(scalars, *refs):
    results = refs[:-6]
    own_ref, swap_ref, lower_ref, held, rows, sem = refs[-6:]
    core, offset, section, lift = scalars[0], scalars[2], scalars[3], scalars[4]
    for tick, result in enumerate(results):

        @pl.when(section == len(results) - tick)
        def _():
            copy = pltpu.make_async_copy(result, held, sem)
            copy.start()
            copy.wait()

    rows[...] = held[...].astype(FLT)
    inner = rows[pl.ds(pl.multiple_of(BAND - offset * WIN, WIN), BAND), :].astype(BF)
    lower, upper = held[0:BAND], held[BAND:SLOT]
    lower_ref[...] = jnp.where(lift == 0, lower, upper)
    even = jnp.where(lift == 0, inner, lower)
    odd = jnp.where(lift == 0, upper, inner)
    own_ref[...] = jnp.where(core == 0, even, odd)
    swap_ref[...] = jnp.where(core == 0, odd, even)


def merge_kernel(
    scalars, own, other, near0, near1, own_last, other_last, forcing, result, rows
):
    core, offset, section, lift = scalars[0], scalars[2], scalars[3], scalars[4]

    @pl.when(section == 0)
    def _():
        for member in range(2):
            mine = jnp.where(
                core == member, own_last[...].astype(FLT), other_last[...].astype(FLT)
            )
            result[member] = mine + forcing[member].astype(FLT)

    @pl.when(section != 0)
    def _():
        for member, near in ((0, near0), (1, near1)):
            mine = BAND * lift
            rows[pl.ds(pl.multiple_of(mine, BAND), BAND), :] = jnp.where(
                core == member, own[...].astype(FLT), other[...].astype(FLT)
            )
            rows[pl.ds(pl.multiple_of(BAND - mine, BAND), BAND), :] = near[...].astype(FLT)
            start = jnp.where(core == 1 - lift, BAND - offset * WIN, mine)
            result[member] = rows[pl.ds(pl.multiple_of(start, WIN), BAND), :]


def struct(shape, kind=BF):
    return jax.ShapeDtypeStruct(shape, kind)


SMEM = pl.BlockSpec(memory_space=pltpu.SMEM)
VMEM = pl.BlockSpec(memory_space=pltpu.VMEM)
ANY = pl.BlockSpec(memory_space=pl.ANY)


def call(name, kernel, scalars, operands, shapes, scratch, place=VMEM, above=()):
    return pl.pallas_call(
        kernel,
        out_shape=shapes,
        in_specs=[SMEM] * (1 + len(above)) + [place] * len(operands),
        out_specs=[VMEM] * len(shapes),
        scratch_shapes=scratch,
        compiler_params=pltpu.CompilerParams(vmem_limit_bytes=40 * 1024 * 1024),
        name=name,
    )(scalars, *above, *operands)


def prepare(scalars, operands, weights, last_slot, above=False, with_forcing=False):
    width, hidden = weights[0].shape
    keys = hidden // HD * SLOT
    shapes = [
        struct((SLOT, keys)),
        struct((SLOT, keys)),
        struct((3, 2 * SLOT, GROUP * SLOT)),
        struct((3, GROUP * SLOT, SLOT)),
        struct((3, SLOT, GROUP * SLOT)),
        struct((SLOT, hidden), FLT),
    ]
    if with_forcing:
        shapes.append(struct((SLOT, width)))
    return call(
        "prepare",
        functools.partial(prepare_kernel, above, with_forcing, last_slot),
        scalars,
        (*operands, *weights[:3]),
        shapes,
        [pltpu.VMEM((3 * BAND, width), FLT)],
    )


def on_device(
    trajectory, observed, obs_mask, shift_rows, final_adjoint, w_query, w_key, w_value, w_out
):
    sections = lax.axis_size("section")
    bands = lax.axis_size("lat")
    chips = bands // 2
    section_at = lax.axis_index("section")
    band_at = lax.axis_index("lat")
    members, rows_here, across, width = trajectory.shape[1:]
    offset = shift_rows[0].astype(jnp.int32)
    core, chip = band_at % 2, band_at // 2
    weights = (w_query[0], w_key[0], w_value[0], w_out[0])

    def at(band, section):
        return (band % bands) * sections + section

    def sent(value, hops):
        return lax.ppermute(value, AXES, hops)

    def moved(ways, among):
        return [(at(a, s), at(b, s)) for a, b in ways for s in among]

    def flat(values):
        return values.reshape(members, 1, BAND, width)

    def ints(*values):
        return jnp.stack(values).astype(jnp.int32)

    last = sections - 1
    x = flat(trajectory[0])
    weight = obs_mask[0].reshape(1, 1, BAND, 1).astype(FLT)
    forcing = (weight * (x.astype(FLT) - flat(observed[0]).astype(FLT))).astype(BF)
    pair = jnp.concatenate([x, forcing], axis=1)
    even_down = [[(2 * j + 2, 2 * j + m) for j in range(chips)] for m in range(2)]
    odd_up = [[(2 * j + 1, 2 * j + 2 + m) for j in range(chips)] for m in range(2)]
    swaps = [(b, b ^ 1) for b in range(bands)]

    def begun(ways):
        run = 2 * RUN
        return [
            (at(a, 0 if a // run != b // run else last), at(b, last)) for a, b in ways
        ]

    with jax.named_scope("first_states"):
        near = [sent(pair[m], moved(odd_up[m], [last])) for m in range(2)]
    with jax.named_scope("first_adjoint"):
        final, _ = lax.optimization_barrier((final_adjoint, pair))
        final = flat(final).astype(BF)
        final_near = [sent(final[m], begun(odd_up[m])) for m in range(2)]
        first_other = sent(
            lax.dynamic_index_in_dim(pair, 1 - core, 0, keepdims=False), moved(swaps, [last])
        )
        final_other = sent(
            lax.dynamic_index_in_dim(final, 1 - core, 0, keepdims=False), moved(swaps, [last])
        )
    lift = jnp.where(section_at == 0, 0, (last - section_at) % 2)
    place = ints(core, chip, offset, section_at, lift)
    prepared = prepare(place, (pair, first_other, *near), weights, chips - 1)
    result = call(
        "first_step",
        first_kernel,
        place,
        (pair, final, first_other, final_other, *near, *final_near, *prepared, *weights),
        [struct((SLOT, width))],
        [pltpu.VMEM((3 * BAND, width), FLT)],
    )
    results = [result[0]]
    with jax.named_scope("later_states"):
        pair_later, _ = lax.optimization_barrier((pair, result[0]))
        rest = list(range(last))
        lifted = [s for s in range(1, last) if (last - s) % 2]
        level = [s for s in rest if s not in lifted]
        later_near = [
            sent(pair_later[m], moved(odd_up[m], level) + moved(even_down[m], lifted))
            for m in range(2)
        ]
        later_other = sent(
            lax.dynamic_index_in_dim(pair_later, 1 - core, 0, keepdims=False),
            moved(swaps, rest),
        )
    with jax.named_scope("shifts"):
        down = [(s, s - 1) for s in range(1, sections)]
        tied, _ = lax.optimization_barrier((shift_rows, later_other))
        above = lax.ppermute(tied, "section", down)
    *prepared, forcing_here = prepare(
        place, (pair, later_other, *later_near), weights, chips - 1, with_forcing=True
    )
    for tick in range(1, sections):
        source = sections - tick
        whole = result[0]

        def across_from(way):
            return [(at(b + 2 * way, source), at(b, source - 1)) for b in range(bands)]

        with jax.named_scope("pass_on"):
            if tick == last:
                from_low = sent(result[1], across_from(-1))
                from_high = sent(whole, across_from(1))
                middle = sent(whole, across_from(0))
                break
            side = sent(whole, across_from(1 if tick % 2 else -1))
            middle = sent(whole, across_from(0))
        shapes = [struct((SLOT, width))]
        if tick == last - 1:
            shapes.append(struct((BAND, width)))
        result = call(
            "step",
            step_kernel,
            place,
            (*((middle, side) if tick % 2 else (side, middle)), *prepared, forcing_here, *weights),
            shapes,
            [pltpu.VMEM((2 * SLOT, width), FLT)],
            above=(above,),
        )
        results.append(result[0])

    with jax.named_scope("window_above"):
        next0, next1 = [sent(x[m], moved(even_down[m], [0])) for m in range(2)]
        extra = prepare(place, (pair, later_other, next0, next1), weights, chips - 1, above=True)
    own, swap, lower = call(
        "split",
        split_kernel,
        place,
        results,
        [struct((BAND, width))] * 3,
        [
            pltpu.VMEM((SLOT, width), BF),
            pltpu.VMEM((SLOT, width), FLT),
            pltpu.SemaphoreType.DMA,
        ],
        place=ANY,
    )
    with jax.named_scope("earlier_results"):
        every = range(1, sections)
        flatly = [s for s in every if s not in lifted]
        near0, near1 = [
            sent(
                lower,
                moved([(2 * j + 2 + m, 2 * j + 1) for j in range(chips)], flatly)
                + moved([(2 * j + m, 2 * j + 2) for j in range(chips)], lifted),
            )
            for m in range(2)
        ]
        other = sent(swap, moved(swaps, every))
    own_last, swap_last = call(
        "last_step",
        last_kernel,
        place,
        (from_low, middle, from_high, *prepared, *extra, *weights),
        [struct((BAND, width))] * 2,
        [pltpu.VMEM((6 * BAND, width), FLT)],
        above=(above,),
    )
    with jax.named_scope("last_result"):
        other_last = sent(swap_last, moved(swaps, [0]))
    (field,) = call(
        "merge",
        merge_kernel,
        place,
        (own, other, near0, near1, own_last, other_last, forcing.reshape(members, BAND, width)),
        [struct((members, BAND, width), FLT)],
        [pltpu.VMEM((SLOT, width), FLT)],
    )
    return field.reshape(1, members, rows_here, across, width)


def solution(mesh):
    placed = (
        P("section", None, "lat", None, None),
        P("section", None, "lat", None, None),
        P("section", "lat", None),
        P("section"),
        P(None, "lat", None, None),
        P("section", None, None),
        P("section", None, None),
        P("section", None, None),
        P("section", None, None),
    )
    return jax.shard_map(
        on_device,
        mesh=mesh,
        in_specs=placed,
        out_specs=P("section", None, "lat", None, None),
        check_vma=False,
    )
```

```python
import functools

import jax
import jax.numpy as jnp
from jax import lax
from jax.experimental import pallas as pl
from jax.experimental.pallas import tpu as pltpu
from jax.sharding import PartitionSpec as P

HD = 32
WIN = 8
AXES = ("lat", "section")
FLT = jnp.float32
BF = jnp.bfloat16
BAND = 64
SLOT = 128
GROUP = 4


def dot_nn(a, b):
    return lax.dot_general(a, b, (((1,), (0,)), ((), ())), preferred_element_type=FLT)


def dot_nt(a, b):
    return lax.dot_general(a, b, (((1,), (1,)), ((), ())), preferred_element_type=FLT)


def near_of(core, near0, near1, field):
    return jnp.where(core == 0, near0[field].astype(FLT), near1[field].astype(FLT))


def gathered(rows, scalars, own, other, near0, near1, field):
    core, offset, lift = scalars[0], scalars[2], scalars[4]

    def place(token, value):
        rows[pl.ds(pl.multiple_of(token, BAND), BAND), :] = value.astype(FLT)

    base = BAND * (1 - lift)
    place(2 * BAND * lift, near_of(core, near0, near1, field))
    place(base + BAND * core, own[core, field])
    place(base + BAND * (1 - core), other[field])
    return rows[pl.ds(pl.multiple_of(offset * WIN, WIN), SLOT), :]


def gathered_above(rows, core, offset, own, other, next0, next1):
    rows[0:BAND, :] = jnp.where(core == 1, own[core, 0].astype(FLT), other[0].astype(FLT))
    rows[BAND : 2 * BAND, :] = near_of(core, next0, next1, 0)
    rows[2 * BAND :, :] = jnp.zeros_like(rows[2 * BAND :, :])
    return rows[pl.ds(pl.multiple_of(offset * WIN, WIN), SLOT), :]


def prepare_kernel(
    above,
    with_forcing,
    last_slot,
    scalars,
    own,
    other,
    near0,
    near1,
    w_query,
    w_key,
    w_value,
    attend_ref,
    attend_t_ref,
    value_ref,
    key_ref,
    query_t_ref,
    out_ref,
    *rest,
):
    rows = rest[-1]
    core, slot, offset = scalars[0], scalars[1], scalars[2]
    if above:
        x = gathered_above(rows, core, offset, own, other, near0, near1).astype(BF)
    else:
        x = gathered(rows, scalars, own, other, near0, near1, 0).astype(BF)
    if with_forcing:
        rest[0][...] = gathered(rows, scalars, own, other, near0, near1, 1).astype(BF)
    scale = HD ** (-0.5)
    q = (dot_nn(x, w_query[...]) * scale).astype(BF)
    k = dot_nn(x, w_key[...]).astype(BF)
    v = dot_nn(x, w_value[...]).astype(BF)
    token = lax.broadcasted_iota(jnp.int32, (SLOT, SLOT), 0)
    other_token = lax.broadcasted_iota(jnp.int32, (SLOT, SLOT), 1)
    row_head = token // HD
    lane_head = other_token // HD
    start = BAND - offset * WIN
    if above:
        edge = jnp.where(slot == last_slot, start, 0)
    else:
        lift = scalars[4]
        edge_slot = jnp.where(lift == 0, 0, last_slot)
        edge = jnp.where(slot == edge_slot, start + BAND * lift, 0)
    allowed = ((token // BAND) == (other_token // BAND)) & (
        (token < edge) == (other_token < edge)
    )
    for group in range(3):
        lanes = slice(SLOT * group, SLOT * group + SLOT)
        q_g, k_g, v_g = q[:, lanes], k[:, lanes], v[:, lanes]
        q_t = q_g.astype(FLT).T
        k_t = k_g.astype(FLT).T
        v_t = v_g.astype(FLT).T
        mixed = jnp.zeros((SLOT, SLOT), FLT)
        for h in range(GROUP):
            at = slice(SLOT * h, SLOT * h + SLOT)
            wide = slice(SLOT * (GROUP * group + h), SLOT * (GROUP * group + h) + SLOT)
            in_rows = row_head == h
            in_lanes = lane_head == h
            scores = dot_nn(q_g, jnp.where(in_rows, k_t, 0.0).astype(BF))
            scores = jnp.where(allowed, scores, -1000000000.0)
            scores = scores - jnp.max(scores, axis=-1, keepdims=True)
            expon = jnp.exp(scores)
            attend = expon / jnp.sum(expon, axis=-1, keepdims=True)
            attend_b = attend.astype(BF)
            attend_ref[:, wide] = attend_b
            attend_t_ref[:, wide] = attend.T.astype(BF)
            mixed += dot_nn(attend_b, jnp.where(in_lanes, v_g, jnp.zeros_like(v_g)))
            value_ref[group, 0:SLOT, at] = jnp.where(in_rows, v_t, 0.0).astype(BF)
            value_ref[group, SLOT : 2 * SLOT, at] = jnp.where(in_rows, -1.0, 0.0).astype(BF)
            key_ref[group, at, :] = jnp.where(in_lanes, k_g, jnp.zeros_like(k_g))
            query_t_ref[group, :, at] = jnp.where(in_rows, q_t, 0.0).astype(BF)
        out_ref[:, lanes] = mixed


def changed(adjoint, units, w_query, w_key, w_value, w_out):
    scale = HD ** (-0.5)
    g = dot_nt(adjoint.astype(BF), w_out[...]).astype(BF)
    lane_head = lax.broadcasted_iota(jnp.int32, (SLOT, SLOT), 1) // HD
    g_query, g_key, g_value = [], [], []
    for unit, (attend, attend_t, values, keys, queries_t, out) in enumerate(units):
        tokens = slice(SLOT * unit, SLOT * unit + SLOT)
        for group in range(3):
            lanes = slice(SLOT * group, SLOT * group + SLOT)
            wide = slice(GROUP * SLOT * group, GROUP * SLOT * (group + 1))
            g_g = g[tokens, lanes]
            g_o = (g_g.astype(FLT) * out[:, lanes]).astype(BF)
            centred = dot_nn(jnp.concatenate([g_g, g_o], axis=1), values[group])
            g_s = (attend[:, wide].astype(FLT) * centred).astype(BF)
            g_query.append((dot_nn(g_s, keys[group]) * scale).astype(BF))
            stacked = jnp.concatenate(
                [g_s[:, SLOT * h : SLOT * h + SLOT] for h in range(GROUP)], axis=0
            )
            g_key.append(dot_nn(queries_t[group], stacked).T.astype(BF))
            spread = jnp.concatenate(
                [jnp.where(lane_head == h, g_g, jnp.zeros_like(g_g)) for h in range(GROUP)],
                axis=0,
            )
            g_value.append(dot_nn(attend_t[:, wide], spread).astype(BF))

    def whole(parts):
        slots = [jnp.concatenate(parts[3 * u : 3 * u + 3], axis=1) for u in range(len(units))]
        return jnp.concatenate(slots, axis=0)

    change = dot_nt(whole(g_query), w_query[...])
    change += dot_nt(whole(g_key), w_key[...])
    change += dot_nt(whole(g_value), w_value[...])
    return change


def shift_kernel(scalars, above, moving):
    for i in range(5):
        moving[i] = scalars[i]
    moving[5] = scalars[2] - above[0]


def first_kernel(scalars, own, other, near0, near1, *refs):
    prepared, weights = refs[:6], refs[6:10]
    all_ref, rows = refs[10:]
    forcing = gathered(rows, scalars, own, other, near0, near1, 1)
    adjoint = gathered(rows, scalars, own, other, near0, near1, 2)
    all_ref[...] = (adjoint + changed(adjoint, [prepared], *weights) + forcing).astype(BF)


def step_kernel(scalars, low, high, *refs):
    prepared, forcing, weights = refs[:6], refs[6], refs[7:11]
    outs, rows = refs[11:-1], refs[-1]
    rows[0:SLOT, :] = low[...].astype(FLT)
    rows[SLOT:, :] = high[...].astype(FLT)
    start = BAND + scalars[5] * WIN
    adjoint = rows[pl.ds(pl.multiple_of(start, WIN), SLOT), :]
    change = changed(adjoint, [prepared], *weights)
    updated = (adjoint + change + forcing[...].astype(FLT)).astype(BF)
    outs[0][...] = updated
    if len(outs) == 2:
        outs[1][...] = updated[BAND:]


def last_kernel(scalars, low, middle, high, *refs):
    units, weights = [refs[:6], refs[6:12]], refs[12:16]
    own_ref, swap_ref, rows = refs[16:]
    rows[0:BAND, :] = low[...].astype(FLT)
    rows[BAND : BAND + SLOT, :] = middle[...].astype(FLT)
    rows[BAND + SLOT : BAND + 2 * SLOT, :] = high[...].astype(FLT)
    rows[BAND + 2 * SLOT :, :] = jnp.zeros_like(rows[BAND + 2 * SLOT :, :])
    core, offset, shift = scalars[0], scalars[2], scalars[5]
    adjoint = rows[pl.ds(pl.multiple_of(BAND + shift * WIN, WIN), 2 * SLOT), :]
    rows[0 : 2 * SLOT, :] = adjoint + changed(adjoint, units, *weights)
    even = rows[pl.ds(pl.multiple_of(BAND - offset * WIN, WIN), BAND), :].astype(BF)
    odd = rows[pl.ds(pl.multiple_of(2 * BAND - offset * WIN, WIN), BAND), :].astype(BF)
    own_ref[...] = jnp.where(core == 0, even, odd)
    swap_ref[...] = jnp.where(core == 0, odd, even)


def split_kernel(scalars, *refs):
    results = refs[:-6]
    own_ref, swap_ref, lower_ref, held, rows, sem = refs[-6:]
    core, offset, section, lift = scalars[0], scalars[2], scalars[3], scalars[4]
    for tick, result in enumerate(results):

        @pl.when(section == len(results) - tick)
        def _():
            copy = pltpu.make_async_copy(result, held, sem)
            copy.start()
            copy.wait()

    rows[...] = held[...].astype(FLT)
    inner = rows[pl.ds(pl.multiple_of(BAND - offset * WIN, WIN), BAND), :].astype(BF)
    lower, upper = held[0:BAND], held[BAND:SLOT]
    lower_ref[...] = jnp.where(lift == 0, lower, upper)
    even = jnp.where(lift == 0, inner, lower)
    odd = jnp.where(lift == 0, upper, inner)
    own_ref[...] = jnp.where(core == 0, even, odd)
    swap_ref[...] = jnp.where(core == 0, odd, even)


def merge_kernel(
    scalars, own, other, near0, near1, own_last, other_last, forcing, result, rows
):
    core, offset, section, lift = scalars[0], scalars[2], scalars[3], scalars[4]

    @pl.when(section == 0)
    def _():
        for member in range(2):
            mine = jnp.where(
                core == member, own_last[...].astype(FLT), other_last[...].astype(FLT)
            )
            result[member] = mine + forcing[member].astype(FLT)

    @pl.when(section != 0)
    def _():
        for member, near in ((0, near0), (1, near1)):
            mine = BAND * lift
            rows[pl.ds(pl.multiple_of(mine, BAND), BAND), :] = jnp.where(
                core == member, own[...].astype(FLT), other[...].astype(FLT)
            )
            rows[pl.ds(pl.multiple_of(BAND - mine, BAND), BAND), :] = near[...].astype(FLT)
            start = jnp.where(core == 1 - lift, BAND - offset * WIN, mine)
            result[member] = rows[pl.ds(pl.multiple_of(start, WIN), BAND), :]


def struct(shape, kind=BF):
    return jax.ShapeDtypeStruct(shape, kind)


SMEM = pl.BlockSpec(memory_space=pltpu.SMEM)
VMEM = pl.BlockSpec(memory_space=pltpu.VMEM)
ANY = pl.BlockSpec(memory_space=pl.ANY)


def call(name, kernel, scalars, operands, shapes, scratch, place=VMEM):
    return pl.pallas_call(
        kernel,
        out_shape=shapes,
        in_specs=[SMEM] + [place] * len(operands),
        out_specs=[VMEM] * len(shapes),
        scratch_shapes=scratch,
        compiler_params=pltpu.CompilerParams(vmem_limit_bytes=40 * 1024 * 1024),
        name=name,
    )(scalars, *operands)


def prepare(scalars, operands, weights, last_slot, above=False, with_forcing=False):
    width, hidden = weights[0].shape
    keys = hidden // HD * SLOT
    shapes = [
        struct((SLOT, keys)),
        struct((SLOT, keys)),
        struct((3, 2 * SLOT, GROUP * SLOT)),
        struct((3, GROUP * SLOT, SLOT)),
        struct((3, SLOT, GROUP * SLOT)),
        struct((SLOT, hidden), FLT),
    ]
    if with_forcing:
        shapes.append(struct((SLOT, width)))
    return call(
        "prepare",
        functools.partial(prepare_kernel, above, with_forcing, last_slot),
        scalars,
        (*operands, *weights[:3]),
        shapes,
        [pltpu.VMEM((3 * BAND, width), FLT)],
    )


def on_device(
    trajectory, observed, obs_mask, shift_rows, final_adjoint, w_query, w_key, w_value, w_out
):
    sections = lax.axis_size("section")
    bands = lax.axis_size("lat")
    chips = bands // 2
    section_at = lax.axis_index("section")
    band_at = lax.axis_index("lat")
    members, rows_here, across, width = trajectory.shape[1:]
    offset = shift_rows[0].astype(jnp.int32)
    core, chip = band_at % 2, band_at // 2
    weights = (w_query[0], w_key[0], w_value[0], w_out[0])

    def at(band, section):
        return (band % bands) * sections + section

    def sent(value, hops):
        return lax.ppermute(value, AXES, hops)

    def moved(ways, among):
        return [(at(a, s), at(b, s)) for a, b in ways for s in among]

    def flat(values):
        return values.reshape(members, 1, BAND, width)

    def ints(*values):
        return jnp.stack(values).astype(jnp.int32)

    last = sections - 1
    x = flat(trajectory[0])
    weight = obs_mask[0].reshape(1, 1, BAND, 1).astype(FLT)
    forcing = (weight * (x.astype(FLT) - flat(observed[0]).astype(FLT))).astype(BF)
    pair = jnp.concatenate([x, forcing], axis=1)
    even_down = [[(2 * j + 2, 2 * j + m) for j in range(chips)] for m in range(2)]
    odd_up = [[(2 * j + 1, 2 * j + 2 + m) for j in range(chips)] for m in range(2)]
    swaps = [(b, b ^ 1) for b in range(bands)]

    begin = jnp.concatenate([pair, flat(final_adjoint).astype(BF)], axis=1)
    with jax.named_scope("first_states"):
        near = [sent(begin[m], moved(odd_up[m], [last])) for m in range(2)]
        first_other = sent(
            lax.dynamic_index_in_dim(begin, 1 - core, 0, keepdims=False), moved(swaps, [last])
        )
    lift = jnp.where(section_at == 0, 0, (last - section_at) % 2)
    place = ints(core, chip, offset, section_at, lift)
    prepared = prepare(place, (begin, first_other, *near), weights, chips - 1)
    result = call(
        "first_step",
        first_kernel,
        place,
        (begin, first_other, *near, *prepared, *weights),
        [struct((SLOT, width))],
        [pltpu.VMEM((3 * BAND, width), FLT)],
    )
    results = [result[0]]
    with jax.named_scope("later_states"):
        pair_later, _ = lax.optimization_barrier((pair, result[0]))
        rest = list(range(last))
        lifted = [s for s in range(1, last) if (last - s) % 2]
        level = [s for s in rest if s not in lifted]
        later_near = [
            sent(pair_later[m], moved(odd_up[m], level) + moved(even_down[m], lifted))
            for m in range(2)
        ]
        later_other = sent(
            lax.dynamic_index_in_dim(pair_later, 1 - core, 0, keepdims=False),
            moved(swaps, rest),
        )
    with jax.named_scope("shifts"):
        down = [(s, s - 1) for s in range(1, sections)]
        tied, _ = lax.optimization_barrier((shift_rows, later_other))
        above = lax.ppermute(tied, "section", down)
        moving = pl.pallas_call(
            shift_kernel,
            out_shape=struct((6,), jnp.int32),
            in_specs=[SMEM] * 2,
            out_specs=SMEM,
            compiler_params=pltpu.CompilerParams(vmem_limit_bytes=64 * 1024),
            name="shift",
        )(place, above)
    *prepared, forcing_here = prepare(
        place, (pair, later_other, *later_near), weights, chips - 1, with_forcing=True
    )
    with jax.named_scope("window_above"):
        x_later, _ = lax.optimization_barrier((x, later_other))
        next0, next1 = [sent(x_later[m], moved(even_down[m], [0])) for m in range(2)]
        extra = prepare(place, (pair, later_other, next0, next1), weights, chips - 1, above=True)
    forcing_here, _ = lax.optimization_barrier((forcing_here, extra[0]))
    for tick in range(1, sections):
        source = sections - tick
        whole = result[0]

        def across_from(way):
            return [(at(b + 2 * way, source), at(b, source - 1)) for b in range(bands)]

        with jax.named_scope("pass_on"):
            if tick == last:
                from_low = sent(result[1], across_from(-1))
                from_high = sent(whole, across_from(1))
                middle = sent(whole, across_from(0))
                break
            side = sent(whole, across_from(1 if tick % 2 else -1))
            middle = sent(whole, across_from(0))
        shapes = [struct((SLOT, width))]
        if tick == last - 1:
            shapes.append(struct((BAND, width)))
        result = call(
            "step",
            step_kernel,
            moving,
            (*((middle, side) if tick % 2 else (side, middle)), *prepared, forcing_here, *weights),
            shapes,
            [pltpu.VMEM((2 * SLOT, width), FLT)],
        )
        results.append(result[0])

    own, swap, lower = call(
        "split",
        split_kernel,
        place,
        results,
        [struct((BAND, width))] * 3,
        [
            pltpu.VMEM((SLOT, width), BF),
            pltpu.VMEM((SLOT, width), FLT),
            pltpu.SemaphoreType.DMA,
        ],
        place=ANY,
    )
    with jax.named_scope("earlier_results"):
        every = range(1, sections)
        flatly = [s for s in every if s not in lifted]
        near0, near1 = [
            sent(
                lower,
                moved([(2 * j + 2 + m, 2 * j + 1) for j in range(chips)], flatly)
                + moved([(2 * j + m, 2 * j + 2) for j in range(chips)], lifted),
            )
            for m in range(2)
        ]
        other = sent(swap, moved(swaps, every))
    own_last, swap_last = call(
        "last_step",
        last_kernel,
        moving,
        (from_low, middle, from_high, *prepared, *extra, *weights),
        [struct((BAND, width))] * 2,
        [pltpu.VMEM((6 * BAND, width), FLT)],
    )
    with jax.named_scope("last_result"):
        other_last = sent(swap_last, moved(swaps, [0]))
    (field,) = call(
        "merge",
        merge_kernel,
        place,
        (own, other, near0, near1, own_last, other_last, forcing.reshape(members, BAND, width)),
        [struct((members, BAND, width), FLT)],
        [pltpu.VMEM((SLOT, width), FLT)],
    )
    return field.reshape(1, members, rows_here, across, width)


def solution(mesh):
    placed = (
        P("section", None, "lat", None, None),
        P("section", None, "lat", None, None),
        P("section", "lat", None),
        P("section"),
        P(None, "lat", None, None),
        P("section", None, None),
        P("section", None, None),
        P("section", None, None),
        P("section", None, None),
    )
    return jax.shard_map(
        on_device,
        mesh=mesh,
        in_specs=placed,
        out_specs=P("section", None, "lat", None, None),
        check_vma=False,
    )
```

```python
import functools

import jax
import jax.numpy as jnp
from jax import lax
from jax.experimental import pallas as pl
from jax.experimental.pallas import tpu as pltpu
from jax.sharding import PartitionSpec as P

HD = 32
WIN = 8
AXES = ("lat", "section")
FLT = jnp.float32
BF = jnp.bfloat16
BAND = 64
SLOT = 128
GROUP = 4


def dot_nn(a, b):
    return lax.dot_general(a, b, (((1,), (0,)), ((), ())), preferred_element_type=FLT)


def dot_nt(a, b):
    return lax.dot_general(a, b, (((1,), (1,)), ((), ())), preferred_element_type=FLT)


def near_of(core, near0, near1, field):
    return jnp.where(core == 0, near0[field].astype(FLT), near1[field].astype(FLT))


def gathered(rows, scalars, own, other, near0, near1, field):
    core, offset, lift = scalars[0], scalars[2], scalars[4]

    def place(token, value):
        rows[pl.ds(pl.multiple_of(token, BAND), BAND), :] = value.astype(FLT)

    base = BAND * (1 - lift)
    place(2 * BAND * lift, near_of(core, near0, near1, field))
    place(base + BAND * core, own[core, field])
    place(base + BAND * (1 - core), other[field])
    return rows[pl.ds(pl.multiple_of(offset * WIN, WIN), SLOT), :]


def gathered_above(rows, core, offset, own, other, next0, next1):
    rows[0:BAND, :] = jnp.where(core == 1, own[core, 0].astype(FLT), other[0].astype(FLT))
    rows[BAND : 2 * BAND, :] = near_of(core, next0, next1, 0)
    rows[2 * BAND :, :] = jnp.zeros_like(rows[2 * BAND :, :])
    return rows[pl.ds(pl.multiple_of(offset * WIN, WIN), SLOT), :]


def prepare_kernel(
    above,
    with_forcing,
    last_slot,
    scalars,
    own,
    other,
    near0,
    near1,
    w_query,
    w_key,
    w_value,
    attend_ref,
    attend_t_ref,
    value_ref,
    key_ref,
    query_t_ref,
    out_ref,
    *rest,
):
    rows = rest[-1]
    core, slot, offset = scalars[0], scalars[1], scalars[2]
    if above:
        x = gathered_above(rows, core, offset, own, other, near0, near1).astype(BF)
    else:
        x = gathered(rows, scalars, own, other, near0, near1, 0).astype(BF)
    if with_forcing:
        rest[0][...] = gathered(rows, scalars, own, other, near0, near1, 1).astype(BF)
    scale = HD ** (-0.5)
    q = (dot_nn(x, w_query[...]) * scale).astype(BF)
    k = dot_nn(x, w_key[...]).astype(BF)
    v = dot_nn(x, w_value[...]).astype(BF)
    token = lax.broadcasted_iota(jnp.int32, (SLOT, SLOT), 0)
    other_token = lax.broadcasted_iota(jnp.int32, (SLOT, SLOT), 1)
    row_head = token // HD
    lane_head = other_token // HD
    start = BAND - offset * WIN
    if above:
        edge = jnp.where(slot == last_slot, start, 0)
    else:
        lift = scalars[4]
        edge_slot = jnp.where(lift == 0, 0, last_slot)
        edge = jnp.where(slot == edge_slot, start + BAND * lift, 0)
    allowed = ((token // BAND) == (other_token // BAND)) & (
        (token < edge) == (other_token < edge)
    )
    for group in range(3):
        lanes = slice(SLOT * group, SLOT * group + SLOT)
        q_g, k_g, v_g = q[:, lanes], k[:, lanes], v[:, lanes]
        q_t = q_g.astype(FLT).T
        k_t = k_g.astype(FLT).T
        v_t = v_g.astype(FLT).T
        mixed = jnp.zeros((SLOT, SLOT), FLT)
        for h in range(GROUP):
            at = slice(SLOT * h, SLOT * h + SLOT)
            wide = slice(SLOT * (GROUP * group + h), SLOT * (GROUP * group + h) + SLOT)
            in_rows = row_head == h
            in_lanes = lane_head == h
            scores = dot_nn(q_g, jnp.where(in_rows, k_t, 0.0).astype(BF))
            scores = jnp.where(allowed, scores, -1000000000.0)
            scores = scores - jnp.max(scores, axis=-1, keepdims=True)
            expon = jnp.exp(scores)
            attend = expon / jnp.sum(expon, axis=-1, keepdims=True)
            attend_b = attend.astype(BF)
            attend_ref[:, wide] = attend_b
            attend_t_ref[:, wide] = attend.T.astype(BF)
            mixed += dot_nn(attend_b, jnp.where(in_lanes, v_g, jnp.zeros_like(v_g)))
            value_ref[group, 0:SLOT, at] = jnp.where(in_rows, v_t, 0.0).astype(BF)
            value_ref[group, SLOT : 2 * SLOT, at] = jnp.where(in_rows, -1.0, 0.0).astype(BF)
            key_ref[group, at, :] = jnp.where(in_lanes, k_g, jnp.zeros_like(k_g))
            query_t_ref[group, :, at] = jnp.where(in_rows, q_t, 0.0).astype(BF)
        out_ref[:, lanes] = mixed


def changed(adjoint, units, w_query, w_key, w_value, w_out):
    scale = HD ** (-0.5)
    g = dot_nt(adjoint.astype(BF), w_out[...]).astype(BF)
    lane_head = lax.broadcasted_iota(jnp.int32, (SLOT, SLOT), 1) // HD
    g_query, g_key, g_value = [], [], []
    for unit, (attend, attend_t, values, keys, queries_t, out) in enumerate(units):
        tokens = slice(SLOT * unit, SLOT * unit + SLOT)
        for group in range(3):
            lanes = slice(SLOT * group, SLOT * group + SLOT)
            wide = slice(GROUP * SLOT * group, GROUP * SLOT * (group + 1))
            g_g = g[tokens, lanes]
            g_o = (g_g.astype(FLT) * out[:, lanes]).astype(BF)
            centred = dot_nn(jnp.concatenate([g_g, g_o], axis=1), values[group])
            g_s = (attend[:, wide].astype(FLT) * centred).astype(BF)
            g_query.append((dot_nn(g_s, keys[group]) * scale).astype(BF))
            stacked = jnp.concatenate(
                [g_s[:, SLOT * h : SLOT * h + SLOT] for h in range(GROUP)], axis=0
            )
            g_key.append(dot_nn(queries_t[group], stacked).T.astype(BF))
            spread = jnp.concatenate(
                [jnp.where(lane_head == h, g_g, jnp.zeros_like(g_g)) for h in range(GROUP)],
                axis=0,
            )
            g_value.append(dot_nn(attend_t[:, wide], spread).astype(BF))

    def whole(parts):
        slots = [jnp.concatenate(parts[3 * u : 3 * u + 3], axis=1) for u in range(len(units))]
        return jnp.concatenate(slots, axis=0)

    change = dot_nt(whole(g_query), w_query[...])
    change += dot_nt(whole(g_key), w_key[...])
    change += dot_nt(whole(g_value), w_value[...])
    return change


def shift_kernel(scalars, above, moving):
    for i in range(5):
        moving[i] = scalars[i]
    moving[5] = scalars[2] - above[0]


def first_kernel(scalars, own, other, near0, near1, *refs):
    prepared, weights = refs[:6], refs[6:10]
    all_ref, rows = refs[10:]
    forcing = gathered(rows, scalars, own, other, near0, near1, 1)
    adjoint = gathered(rows, scalars, own, other, near0, near1, 2)
    all_ref[...] = (adjoint + changed(adjoint, [prepared], *weights) + forcing).astype(BF)


def step_kernel(scalars, low, high, *refs):
    prepared, forcing, weights = refs[:6], refs[6], refs[7:11]
    outs, rows = refs[11:-1], refs[-1]
    rows[0:SLOT, :] = low[...].astype(FLT)
    rows[SLOT:, :] = high[...].astype(FLT)
    start = BAND + scalars[5] * WIN
    adjoint = rows[pl.ds(pl.multiple_of(start, WIN), SLOT), :]
    change = changed(adjoint, [prepared], *weights)
    updated = (adjoint + change + forcing[...].astype(FLT)).astype(BF)
    outs[0][...] = updated
    if len(outs) == 2:
        outs[1][...] = updated[BAND:]


def last_kernel(scalars, low, middle, high, *refs):
    units, weights = [refs[:6], refs[6:12]], refs[12:16]
    own_ref, swap_ref, rows = refs[16:]
    rows[0:BAND, :] = low[...].astype(FLT)
    rows[BAND : BAND + SLOT, :] = middle[...].astype(FLT)
    rows[BAND + SLOT : BAND + 2 * SLOT, :] = high[...].astype(FLT)
    rows[BAND + 2 * SLOT :, :] = jnp.zeros_like(rows[BAND + 2 * SLOT :, :])
    core, offset, shift = scalars[0], scalars[2], scalars[5]
    adjoint = rows[pl.ds(pl.multiple_of(BAND + shift * WIN, WIN), 2 * SLOT), :]
    rows[0 : 2 * SLOT, :] = adjoint + changed(adjoint, units, *weights)
    even = rows[pl.ds(pl.multiple_of(BAND - offset * WIN, WIN), BAND), :].astype(BF)
    odd = rows[pl.ds(pl.multiple_of(2 * BAND - offset * WIN, WIN), BAND), :].astype(BF)
    own_ref[...] = jnp.where(core == 0, even, odd)
    swap_ref[...] = jnp.where(core == 0, odd, even)


def split_kernel(scalars, *refs):
    results = refs[:-6]
    own_ref, swap_ref, lower_ref, held, rows, sem = refs[-6:]
    core, offset, section, lift = scalars[0], scalars[2], scalars[3], scalars[4]
    for tick, result in enumerate(results):

        @pl.when(section == len(results) - tick)
        def _():
            copy = pltpu.make_async_copy(result, held, sem)
            copy.start()
            copy.wait()

    rows[...] = held[...].astype(FLT)
    inner = rows[pl.ds(pl.multiple_of(BAND - offset * WIN, WIN), BAND), :].astype(BF)
    lower, upper = held[0:BAND], held[BAND:SLOT]
    lower_ref[...] = jnp.where(lift == 0, lower, upper)
    even = jnp.where(lift == 0, inner, lower)
    odd = jnp.where(lift == 0, upper, inner)
    own_ref[...] = jnp.where(core == 0, even, odd)
    swap_ref[...] = jnp.where(core == 0, odd, even)


def merge_kernel(
    scalars, own, other, near0, near1, own_last, other_last, forcing, result, rows
):
    core, offset, section, lift = scalars[0], scalars[2], scalars[3], scalars[4]

    @pl.when(section == 0)
    def _():
        for member in range(2):
            mine = jnp.where(
                core == member, own_last[...].astype(FLT), other_last[...].astype(FLT)
            )
            result[member] = mine + forcing[member].astype(FLT)

    @pl.when(section != 0)
    def _():
        for member, near in ((0, near0), (1, near1)):
            mine = BAND * lift
            rows[pl.ds(pl.multiple_of(mine, BAND), BAND), :] = jnp.where(
                core == member, own[...].astype(FLT), other[...].astype(FLT)
            )
            rows[pl.ds(pl.multiple_of(BAND - mine, BAND), BAND), :] = near[...].astype(FLT)
            start = jnp.where(core == 1 - lift, BAND - offset * WIN, mine)
            result[member] = rows[pl.ds(pl.multiple_of(start, WIN), BAND), :]


def struct(shape, kind=BF):
    return jax.ShapeDtypeStruct(shape, kind)


SMEM = pl.BlockSpec(memory_space=pltpu.SMEM)
VMEM = pl.BlockSpec(memory_space=pltpu.VMEM)
ANY = pl.BlockSpec(memory_space=pl.ANY)


def gated(kernel, section):
    def body(scalars, *refs):
        @pl.when(scalars[3] == section)
        def _():
            kernel(scalars, *refs)

    return body


def call(name, kernel, scalars, operands, shapes, scratch, place=VMEM, only=None):
    if only is not None:
        kernel = gated(kernel, only)
    return pl.pallas_call(
        kernel,
        out_shape=shapes,
        in_specs=[SMEM] + [place] * len(operands),
        out_specs=[VMEM] * len(shapes),
        scratch_shapes=scratch,
        compiler_params=pltpu.CompilerParams(vmem_limit_bytes=40 * 1024 * 1024),
        name=name,
    )(scalars, *operands)


def prepare(scalars, operands, weights, last_slot, above=False, with_forcing=False, only=None):
    width, hidden = weights[0].shape
    keys = hidden // HD * SLOT
    shapes = [
        struct((SLOT, keys)),
        struct((SLOT, keys)),
        struct((3, 2 * SLOT, GROUP * SLOT)),
        struct((3, GROUP * SLOT, SLOT)),
        struct((3, SLOT, GROUP * SLOT)),
        struct((SLOT, hidden), FLT),
    ]
    if with_forcing:
        shapes.append(struct((SLOT, width)))
    return call(
        "prepare",
        functools.partial(prepare_kernel, above, with_forcing, last_slot),
        scalars,
        (*operands, *weights[:3]),
        shapes,
        [pltpu.VMEM((3 * BAND, width), FLT)],
        only=only,
    )


def on_device(
    trajectory, observed, obs_mask, shift_rows, final_adjoint, w_query, w_key, w_value, w_out
):
    sections = lax.axis_size("section")
    bands = lax.axis_size("lat")
    chips = bands // 2
    section_at = lax.axis_index("section")
    band_at = lax.axis_index("lat")
    members, rows_here, across, width = trajectory.shape[1:]
    offset = shift_rows[0].astype(jnp.int32)
    core, chip = band_at % 2, band_at // 2
    weights = (w_query[0], w_key[0], w_value[0], w_out[0])

    def at(band, section):
        return (band % bands) * sections + section

    def sent(value, hops):
        return lax.ppermute(value, AXES, hops)

    def moved(ways, among):
        return [(at(a, s), at(b, s)) for a, b in ways for s in among]

    def flat(values):
        return values.reshape(members, 1, BAND, width)

    def ints(*values):
        return jnp.stack(values).astype(jnp.int32)

    last = sections - 1
    x = flat(trajectory[0])
    weight = obs_mask[0].reshape(1, 1, BAND, 1).astype(FLT)
    forcing = (weight * (x.astype(FLT) - flat(observed[0]).astype(FLT))).astype(BF)
    pair = jnp.concatenate([x, forcing], axis=1)
    even_down = [[(2 * j + 2, 2 * j + m) for j in range(chips)] for m in range(2)]
    odd_up = [[(2 * j + 1, 2 * j + 2 + m) for j in range(chips)] for m in range(2)]
    swaps = [(b, b ^ 1) for b in range(bands)]

    begin = jnp.concatenate([pair, flat(final_adjoint).astype(BF)], axis=1)
    with jax.named_scope("first_states"):
        near = [sent(begin[m], moved(odd_up[m], [last])) for m in range(2)]
        first_other = sent(
            lax.dynamic_index_in_dim(begin, 1 - core, 0, keepdims=False), moved(swaps, [last])
        )
    lift = jnp.where(section_at == 0, 0, (last - section_at) % 2)
    place = ints(core, chip, offset, section_at, lift)
    prepared = prepare(place, (begin, first_other, *near), weights, chips - 1, only=last)
    result = call(
        "first_step",
        first_kernel,
        place,
        (begin, first_other, *near, *prepared, *weights),
        [struct((SLOT, width))],
        [pltpu.VMEM((3 * BAND, width), FLT)],
        only=last,
    )
    results = [result[0]]
    with jax.named_scope("later_states"):
        pair_later, _ = lax.optimization_barrier((pair, result[0]))
        rest = list(range(last))
        lifted = [s for s in range(1, last) if (last - s) % 2]
        level = [s for s in rest if s not in lifted]
        later_near = [
            sent(pair_later[m], moved(odd_up[m], level) + moved(even_down[m], lifted))
            for m in range(2)
        ]
        later_other = sent(
            lax.dynamic_index_in_dim(pair_later, 1 - core, 0, keepdims=False),
            moved(swaps, rest),
        )
    with jax.named_scope("shifts"):
        down = [(s, s - 1) for s in range(1, sections)]
        tied, _ = lax.optimization_barrier((shift_rows, later_other))
        above = lax.ppermute(tied, "section", down)
        moving = pl.pallas_call(
            shift_kernel,
            out_shape=struct((6,), jnp.int32),
            in_specs=[SMEM] * 2,
            out_specs=SMEM,
            compiler_params=pltpu.CompilerParams(vmem_limit_bytes=64 * 1024),
            name="shift",
        )(place, above)
    *prepared, forcing_here = prepare(
        place, (pair, later_other, *later_near), weights, chips - 1, with_forcing=True
    )
    with jax.named_scope("window_above"):
        x_later, _ = lax.optimization_barrier((x, later_other))
        next0, next1 = [sent(x_later[m], moved(even_down[m], [0])) for m in range(2)]
        extra = prepare(place, (pair, later_other, next0, next1), weights, chips - 1, above=True, only=0)
    forcing_here, _ = lax.optimization_barrier((forcing_here, extra[0]))
    for tick in range(1, sections):
        source = sections - tick
        whole = result[0]

        def across_from(way):
            return [(at(b + 2 * way, source), at(b, source - 1)) for b in range(bands)]

        with jax.named_scope("pass_on"):
            if tick == last:
                from_low = sent(result[1], across_from(-1))
                from_high = sent(whole, across_from(1))
                middle = sent(whole, across_from(0))
                break
            side = sent(whole, across_from(1 if tick % 2 else -1))
            middle = sent(whole, across_from(0))
        shapes = [struct((SLOT, width))]
        if tick == last - 1:
            shapes.append(struct((BAND, width)))
        result = call(
            "step",
            step_kernel,
            moving,
            (*((middle, side) if tick % 2 else (side, middle)), *prepared, forcing_here, *weights),
            shapes,
            [pltpu.VMEM((2 * SLOT, width), FLT)],
        )
        results.append(result[0])

    own, swap, lower = call(
        "split",
        split_kernel,
        place,
        results,
        [struct((BAND, width))] * 3,
        [
            pltpu.VMEM((SLOT, width), BF),
            pltpu.VMEM((SLOT, width), FLT),
            pltpu.SemaphoreType.DMA,
        ],
        place=ANY,
    )
    with jax.named_scope("earlier_results"):
        every = range(1, sections)
        flatly = [s for s in every if s not in lifted]
        near0, near1 = [
            sent(
                lower,
                moved([(2 * j + 2 + m, 2 * j + 1) for j in range(chips)], flatly)
                + moved([(2 * j + m, 2 * j + 2) for j in range(chips)], lifted),
            )
            for m in range(2)
        ]
        other = sent(swap, moved(swaps, every))
    own_last, swap_last = call(
        "last_step",
        last_kernel,
        moving,
        (from_low, middle, from_high, *prepared, *extra, *weights),
        [struct((BAND, width))] * 2,
        [pltpu.VMEM((6 * BAND, width), FLT)],
    )
    with jax.named_scope("last_result"):
        other_last = sent(swap_last, moved(swaps, [0]))
    (field,) = call(
        "merge",
        merge_kernel,
        place,
        (own, other, near0, near1, own_last, other_last, forcing.reshape(members, BAND, width)),
        [struct((members, BAND, width), FLT)],
        [pltpu.VMEM((SLOT, width), FLT)],
    )
    return field.reshape(1, members, rows_here, across, width)


def solution(mesh):
    placed = (
        P("section", None, "lat", None, None),
        P("section", None, "lat", None, None),
        P("section", "lat", None),
        P("section"),
        P(None, "lat", None, None),
        P("section", None, None),
        P("section", None, None),
        P("section", None, None),
        P("section", None, None),
    )
    return jax.shard_map(
        on_device,
        mesh=mesh,
        in_specs=placed,
        out_specs=P("section", None, "lat", None, None),
        check_vma=False,
    )
```

```python
import functools

import jax
import jax.numpy as jnp
from jax import lax
from jax.experimental import pallas as pl
from jax.experimental.pallas import tpu as pltpu
from jax.sharding import PartitionSpec as P

HD = 32
WIN = 8
AXES = ("lat", "section")
FLT = jnp.float32
BF = jnp.bfloat16
BAND = 64
SLOT = 128
GROUP = 4


def dot_nn(a, b):
    return lax.dot_general(a, b, (((1,), (0,)), ((), ())), preferred_element_type=FLT)


def dot_nt(a, b):
    return lax.dot_general(a, b, (((1,), (1,)), ((), ())), preferred_element_type=FLT)


def near_of(core, near0, near1, field):
    return jnp.where(core == 0, near0[field].astype(FLT), near1[field].astype(FLT))


def gathered(rows, scalars, own, other, near0, near1, field):
    core, offset, lift = scalars[0], scalars[2], scalars[4]

    def place(token, value):
        rows[pl.ds(pl.multiple_of(token, BAND), BAND), :] = value.astype(FLT)

    base = BAND * (1 - lift)
    place(2 * BAND * lift, near_of(core, near0, near1, field))
    place(base + BAND * core, own[core, field])
    place(base + BAND * (1 - core), other[field])
    return rows[pl.ds(pl.multiple_of(offset * WIN, WIN), SLOT), :]


def gathered_above(rows, core, offset, own, other, next0, next1):
    rows[0:BAND, :] = jnp.where(core == 1, own[core, 0].astype(FLT), other[0].astype(FLT))
    rows[BAND : 2 * BAND, :] = near_of(core, next0, next1, 0)
    rows[2 * BAND :, :] = jnp.zeros_like(rows[2 * BAND :, :])
    return rows[pl.ds(pl.multiple_of(offset * WIN, WIN), SLOT), :]


def prepare_kernel(
    above,
    with_forcing,
    last_slot,
    scalars,
    own,
    near0,
    near1,
    other,
    w_query,
    w_key,
    w_value,
    attend_ref,
    attend_t_ref,
    value_ref,
    key_ref,
    query_t_ref,
    out_ref,
    *rest,
):
    rows = rest[-1]
    core, slot, offset = scalars[0], scalars[1], scalars[2]
    if above:
        x = gathered_above(rows, core, offset, own, other, near0, near1).astype(BF)
    else:
        x = gathered(rows, scalars, own, other, near0, near1, 0).astype(BF)
    if with_forcing:
        rest[0][...] = gathered(rows, scalars, own, other, near0, near1, 1).astype(BF)
    scale = HD ** (-0.5)
    q = (dot_nn(x, w_query[...]) * scale).astype(BF)
    k = dot_nn(x, w_key[...]).astype(BF)
    v = dot_nn(x, w_value[...]).astype(BF)
    token = lax.broadcasted_iota(jnp.int32, (SLOT, SLOT), 0)
    other_token = lax.broadcasted_iota(jnp.int32, (SLOT, SLOT), 1)
    row_head = token // HD
    lane_head = other_token // HD
    start = BAND - offset * WIN
    if above:
        edge = jnp.where(slot == last_slot, start, 0)
    else:
        lift = scalars[4]
        edge_slot = jnp.where(lift == 0, 0, last_slot)
        edge = jnp.where(slot == edge_slot, start + BAND * lift, 0)
    allowed = ((token // BAND) == (other_token // BAND)) & (
        (token < edge) == (other_token < edge)
    )
    for group in range(3):
        lanes = slice(SLOT * group, SLOT * group + SLOT)
        q_g, k_g, v_g = q[:, lanes], k[:, lanes], v[:, lanes]
        q_t = q_g.astype(FLT).T
        k_t = k_g.astype(FLT).T
        v_t = v_g.astype(FLT).T
        mixed = jnp.zeros((SLOT, SLOT), FLT)
        for h in range(GROUP):
            at = slice(SLOT * h, SLOT * h + SLOT)
            wide = slice(SLOT * (GROUP * group + h), SLOT * (GROUP * group + h) + SLOT)
            in_rows = row_head == h
            in_lanes = lane_head == h
            scores = dot_nn(q_g, jnp.where(in_rows, k_t, 0.0).astype(BF))
            scores = jnp.where(allowed, scores, -1000000000.0)
            scores = scores - jnp.max(scores, axis=-1, keepdims=True)
            expon = jnp.exp(scores)
            attend = expon / jnp.sum(expon, axis=-1, keepdims=True)
            attend_b = attend.astype(BF)
            attend_ref[:, wide] = attend_b
            attend_t_ref[:, wide] = attend.T.astype(BF)
            mixed += dot_nn(attend_b, jnp.where(in_lanes, v_g, jnp.zeros_like(v_g)))
            value_ref[group, 0:SLOT, at] = jnp.where(in_rows, v_t, 0.0).astype(BF)
            value_ref[group, SLOT : 2 * SLOT, at] = jnp.where(in_rows, -1.0, 0.0).astype(BF)
            key_ref[group, at, :] = jnp.where(in_lanes, k_g, jnp.zeros_like(k_g))
            query_t_ref[group, :, at] = jnp.where(in_rows, q_t, 0.0).astype(BF)
        out_ref[:, lanes] = mixed


def changed(adjoint, units, w_query, w_key, w_value, w_out):
    scale = HD ** (-0.5)
    g = dot_nt(adjoint.astype(BF), w_out[...]).astype(BF)
    lane_head = lax.broadcasted_iota(jnp.int32, (SLOT, SLOT), 1) // HD
    g_query, g_key, g_value = [], [], []
    for unit, (attend, attend_t, values, keys, queries_t, out) in enumerate(units):
        tokens = slice(SLOT * unit, SLOT * unit + SLOT)
        for group in range(3):
            lanes = slice(SLOT * group, SLOT * group + SLOT)
            wide = slice(GROUP * SLOT * group, GROUP * SLOT * (group + 1))
            g_g = g[tokens, lanes]
            g_o = (g_g.astype(FLT) * out[:, lanes]).astype(BF)
            centred = dot_nn(jnp.concatenate([g_g, g_o], axis=1), values[group])
            g_s = (attend[:, wide].astype(FLT) * centred).astype(BF)
            g_query.append((dot_nn(g_s, keys[group]) * scale).astype(BF))
            stacked = jnp.concatenate(
                [g_s[:, SLOT * h : SLOT * h + SLOT] for h in range(GROUP)], axis=0
            )
            g_key.append(dot_nn(queries_t[group], stacked).T.astype(BF))
            spread = jnp.concatenate(
                [jnp.where(lane_head == h, g_g, jnp.zeros_like(g_g)) for h in range(GROUP)],
                axis=0,
            )
            g_value.append(dot_nn(attend_t[:, wide], spread).astype(BF))

    def whole(parts):
        slots = [jnp.concatenate(parts[3 * u : 3 * u + 3], axis=1) for u in range(len(units))]
        return jnp.concatenate(slots, axis=0)

    change = dot_nt(whole(g_query), w_query[...])
    change += dot_nt(whole(g_key), w_key[...])
    change += dot_nt(whole(g_value), w_value[...])
    return change


def shift_kernel(scalars, above, moving):
    for i in range(5):
        moving[i] = scalars[i]
    moving[5] = scalars[2] - above[0]


def first_kernel(scalars, own, near0, near1, other, *refs):
    prepared, weights = refs[:6], refs[6:10]
    all_ref, rows = refs[10:]
    forcing = gathered(rows, scalars, own, other, near0, near1, 1)
    adjoint = gathered(rows, scalars, own, other, near0, near1, 2)
    all_ref[...] = (adjoint + changed(adjoint, [prepared], *weights) + forcing).astype(BF)


def step_kernel(scalars, low, high, *refs):
    prepared, forcing, weights = refs[:6], refs[6], refs[7:11]
    outs, rows = refs[11:-1], refs[-1]
    rows[0:SLOT, :] = low[...].astype(FLT)
    rows[SLOT:, :] = high[...].astype(FLT)
    start = BAND + scalars[5] * WIN
    adjoint = rows[pl.ds(pl.multiple_of(start, WIN), SLOT), :]
    change = changed(adjoint, [prepared], *weights)
    updated = (adjoint + change + forcing[...].astype(FLT)).astype(BF)
    outs[0][...] = updated
    if len(outs) == 2:
        outs[1][...] = updated[BAND:]


def last_kernel(scalars, low, middle, high, *refs):
    units, weights = [refs[:6], refs[6:12]], refs[12:16]
    own_ref, swap_ref, rows = refs[16:]
    rows[0:BAND, :] = low[...].astype(FLT)
    rows[BAND : BAND + SLOT, :] = middle[...].astype(FLT)
    rows[BAND + SLOT : BAND + 2 * SLOT, :] = high[...].astype(FLT)
    rows[BAND + 2 * SLOT :, :] = jnp.zeros_like(rows[BAND + 2 * SLOT :, :])
    core, offset, shift = scalars[0], scalars[2], scalars[5]
    adjoint = rows[pl.ds(pl.multiple_of(BAND + shift * WIN, WIN), 2 * SLOT), :]
    rows[0 : 2 * SLOT, :] = adjoint + changed(adjoint, units, *weights)
    even = rows[pl.ds(pl.multiple_of(BAND - offset * WIN, WIN), BAND), :].astype(BF)
    odd = rows[pl.ds(pl.multiple_of(2 * BAND - offset * WIN, WIN), BAND), :].astype(BF)
    own_ref[...] = jnp.where(core == 0, even, odd)
    swap_ref[...] = jnp.where(core == 0, odd, even)


def split_kernel(scalars, *refs):
    results = refs[:-6]
    own_ref, swap_ref, lower_ref, held, rows, sem = refs[-6:]
    core, offset, section, lift = scalars[0], scalars[2], scalars[3], scalars[4]
    for tick, result in enumerate(results):

        @pl.when(section == len(results) - tick)
        def _():
            copy = pltpu.make_async_copy(result, held, sem)
            copy.start()
            copy.wait()

    rows[...] = held[...].astype(FLT)
    inner = rows[pl.ds(pl.multiple_of(BAND - offset * WIN, WIN), BAND), :].astype(BF)
    lower, upper = held[0:BAND], held[BAND:SLOT]
    lower_ref[...] = jnp.where(lift == 0, lower, upper)
    even = jnp.where(lift == 0, inner, lower)
    odd = jnp.where(lift == 0, upper, inner)
    own_ref[...] = jnp.where(core == 0, even, odd)
    swap_ref[...] = jnp.where(core == 0, odd, even)


def merge_kernel(
    scalars, own, other, near0, near1, own_last, other_last, forcing, result, rows
):
    core, offset, section, lift = scalars[0], scalars[2], scalars[3], scalars[4]

    @pl.when(section == 0)
    def _():
        for member in range(2):
            mine = jnp.where(
                core == member, own_last[...].astype(FLT), other_last[...].astype(FLT)
            )
            result[member] = mine + forcing[member].astype(FLT)

    @pl.when(section != 0)
    def _():
        for member, near in ((0, near0), (1, near1)):
            mine = BAND * lift
            rows[pl.ds(pl.multiple_of(mine, BAND), BAND), :] = jnp.where(
                core == member, own[...].astype(FLT), other[...].astype(FLT)
            )
            rows[pl.ds(pl.multiple_of(BAND - mine, BAND), BAND), :] = near[...].astype(FLT)
            start = jnp.where(core == 1 - lift, BAND - offset * WIN, mine)
            result[member] = rows[pl.ds(pl.multiple_of(start, WIN), BAND), :]


def struct(shape, kind=BF):
    return jax.ShapeDtypeStruct(shape, kind)


SMEM = pl.BlockSpec(memory_space=pltpu.SMEM)
VMEM = pl.BlockSpec(memory_space=pltpu.VMEM)
ANY = pl.BlockSpec(memory_space=pl.ANY)


def gated(kernel, section):
    def body(scalars, *refs):
        @pl.when(scalars[3] == section)
        def _():
            kernel(scalars, *refs)

    return body


def call(name, kernel, scalars, operands, shapes, scratch, place=VMEM, only=None):
    if only is not None:
        kernel = gated(kernel, only)
    return pl.pallas_call(
        kernel,
        out_shape=shapes,
        in_specs=[SMEM] + [place] * len(operands),
        out_specs=[VMEM] * len(shapes),
        scratch_shapes=scratch,
        compiler_params=pltpu.CompilerParams(vmem_limit_bytes=40 * 1024 * 1024),
        name=name,
    )(scalars, *operands)


def prepare(scalars, operands, weights, last_slot, above=False, with_forcing=False, only=None):
    width, hidden = weights[0].shape
    keys = hidden // HD * SLOT
    shapes = [
        struct((SLOT, keys)),
        struct((SLOT, keys)),
        struct((3, 2 * SLOT, GROUP * SLOT)),
        struct((3, GROUP * SLOT, SLOT)),
        struct((3, SLOT, GROUP * SLOT)),
        struct((SLOT, hidden), FLT),
    ]
    if with_forcing:
        shapes.append(struct((SLOT, width)))
    return call(
        "prepare",
        functools.partial(prepare_kernel, above, with_forcing, last_slot),
        scalars,
        (*operands, *weights[:3]),
        shapes,
        [pltpu.VMEM((3 * BAND, width), FLT)],
        only=only,
    )


def on_device(
    trajectory, observed, obs_mask, shift_rows, final_adjoint, w_query, w_key, w_value, w_out
):
    sections = lax.axis_size("section")
    bands = lax.axis_size("lat")
    chips = bands // 2
    section_at = lax.axis_index("section")
    band_at = lax.axis_index("lat")
    members, rows_here, across, width = trajectory.shape[1:]
    offset = shift_rows[0].astype(jnp.int32)
    core, chip = band_at % 2, band_at // 2
    weights = (w_query[0], w_key[0], w_value[0], w_out[0])

    def at(band, section):
        return (band % bands) * sections + section

    def sent(value, hops):
        return lax.ppermute(value, AXES, hops)

    def moved(ways, among):
        return [(at(a, s), at(b, s)) for a, b in ways for s in among]

    def flat(values):
        return values.reshape(members, 1, BAND, width)

    def ints(*values):
        return jnp.stack(values).astype(jnp.int32)

    last = sections - 1
    x = flat(trajectory[0])
    weight = obs_mask[0].reshape(1, 1, BAND, 1).astype(FLT)
    forcing = (weight * (x.astype(FLT) - flat(observed[0]).astype(FLT))).astype(BF)
    pair = jnp.concatenate([x, forcing], axis=1)
    even_down = [[(2 * j + 2, 2 * j + m) for j in range(chips)] for m in range(2)]
    odd_up = [[(2 * j + 1, 2 * j + 2 + m) for j in range(chips)] for m in range(2)]
    swaps = [(b, b ^ 1) for b in range(bands)]

    begin = jnp.concatenate([pair, flat(final_adjoint).astype(BF)], axis=1)
    with jax.named_scope("first_states"):
        near = [sent(begin[m], moved(odd_up[m], [last])) for m in range(2)]
        first_other = sent(
            lax.dynamic_index_in_dim(begin, 1 - core, 0, keepdims=False), moved(swaps, [last])
        )
    lift = jnp.where(section_at == 0, 0, (last - section_at) % 2)
    place = ints(core, chip, offset, section_at, lift)
    prepared = prepare(place, (begin, *near, first_other), weights, chips - 1, only=last)
    result = call(
        "first_step",
        first_kernel,
        place,
        (begin, *near, first_other, *prepared, *weights),
        [struct((SLOT, width))],
        [pltpu.VMEM((3 * BAND, width), FLT)],
        only=last,
    )
    results = [result[0]]
    with jax.named_scope("later_states"):
        pair_later, _ = lax.optimization_barrier((pair, result[0]))
        rest = list(range(last))
        lifted = [s for s in range(1, last) if (last - s) % 2]
        level = [s for s in rest if s not in lifted]
        later_near = [
            sent(pair_later[m], moved(odd_up[m], level) + moved(even_down[m], lifted))
            for m in range(2)
        ]
        later_other = sent(
            lax.dynamic_index_in_dim(pair_later, 1 - core, 0, keepdims=False),
            moved(swaps, rest),
        )
    with jax.named_scope("shifts"):
        down = [(s, s - 1) for s in range(1, sections)]
        tied, _ = lax.optimization_barrier((shift_rows, later_other))
        above = lax.ppermute(tied, "section", down)
        moving = pl.pallas_call(
            shift_kernel,
            out_shape=struct((6,), jnp.int32),
            in_specs=[SMEM] * 2,
            out_specs=SMEM,
            compiler_params=pltpu.CompilerParams(vmem_limit_bytes=64 * 1024),
            name="shift",
        )(place, above)
    *prepared, forcing_here = prepare(
        place, (pair, *later_near, later_other), weights, chips - 1, with_forcing=True
    )
    with jax.named_scope("window_above"):
        x_later, _ = lax.optimization_barrier((x, later_other))
        next0, next1 = [sent(x_later[m], moved(even_down[m], [0])) for m in range(2)]
        extra = prepare(place, (pair, next0, next1, later_other), weights, chips - 1, above=True, only=0)
    forcing_here, _ = lax.optimization_barrier((forcing_here, extra[0]))
    for tick in range(1, sections):
        source = sections - tick
        whole = result[0]

        def across_from(way):
            return [(at(b + 2 * way, source), at(b, source - 1)) for b in range(bands)]

        with jax.named_scope("pass_on"):
            if tick == last:
                from_low = sent(result[1], across_from(-1))
                from_high = sent(whole, across_from(1))
                middle = sent(whole, across_from(0))
                break
            side = sent(whole, across_from(1 if tick % 2 else -1))
            middle = sent(whole, across_from(0))
        shapes = [struct((SLOT, width))]
        if tick == last - 1:
            shapes.append(struct((BAND, width)))
        result = call(
            "step",
            step_kernel,
            moving,
            (*((middle, side) if tick % 2 else (side, middle)), *prepared, forcing_here, *weights),
            shapes,
            [pltpu.VMEM((2 * SLOT, width), FLT)],
        )
        results.append(result[0])

    own, swap, lower = call(
        "split",
        split_kernel,
        place,
        results,
        [struct((BAND, width))] * 3,
        [
            pltpu.VMEM((SLOT, width), BF),
            pltpu.VMEM((SLOT, width), FLT),
            pltpu.SemaphoreType.DMA,
        ],
        place=ANY,
    )
    with jax.named_scope("earlier_results"):
        every = range(1, sections)
        flatly = [s for s in every if s not in lifted]
        near0, near1 = [
            sent(
                lower,
                moved([(2 * j + 2 + m, 2 * j + 1) for j in range(chips)], flatly)
                + moved([(2 * j + m, 2 * j + 2) for j in range(chips)], lifted),
            )
            for m in range(2)
        ]
        other = sent(swap, moved(swaps, every))
    own_last, swap_last = call(
        "last_step",
        last_kernel,
        moving,
        (from_low, middle, from_high, *prepared, *extra, *weights),
        [struct((BAND, width))] * 2,
        [pltpu.VMEM((6 * BAND, width), FLT)],
    )
    with jax.named_scope("last_result"):
        other_last = sent(swap_last, moved(swaps, [0]))
    (field,) = call(
        "merge",
        merge_kernel,
        place,
        (own, other, near0, near1, own_last, other_last, forcing.reshape(members, BAND, width)),
        [struct((members, BAND, width), FLT)],
        [pltpu.VMEM((SLOT, width), FLT)],
    )
    return field.reshape(1, members, rows_here, across, width)


def solution(mesh):
    placed = (
        P("section", None, "lat", None, None),
        P("section", None, "lat", None, None),
        P("section", "lat", None),
        P("section"),
        P(None, "lat", None, None),
        P("section", None, None),
        P("section", None, None),
        P("section", None, None),
        P("section", None, None),
    )
    return jax.shard_map(
        on_device,
        mesh=mesh,
        in_specs=placed,
        out_specs=P("section", None, "lat", None, None),
        check_vma=False,
    )
```
